256 devices in a mesh: row: 32 (over y, x, core), col: 8 (over z).
Axes of the slice: x: 4, y: 4, z: 8, core: 2. Of those that a mesh axis runs over, the one named last changes fastest.
Arguments:
- tokens: bfloat16 [8192, 4096], P('row', 'col'), may hold values from -6 to 6
- contig_lengths: int32 [64], replicated, may hold values from 1 to 768, 8192 in all
- w_in: bfloat16 [4096, 4096], P('row', 'col'), may hold values from -0.09375 to 0.09375
- conv_filter: float32 [128, 4096], P(None, 'col'), may hold values from -0.5 to 0.5
- d_gated: bfloat16 [8192, 4096], P('row', 'col'), may hold values from -6 to 6
Outputs:
- gated: bfloat16 [8192, 4096], P('row', 'col')
- d_tokens: bfloat16 [8192, 4096], P('row', 'col')
- grad_in: float32 [4096, 4096], P('row', 'col')
The draws below stay inside these ranges and needn't reach their ends.
Inputs may be any that keep to these rules, and one draw needn't show every extreme that they name: `contig_lengths`: the 64 lengths sum to 8192; the longest is exactly 768.
All inputs are finite; a program needn't handle non-finite values.
Results may differ from the reference program's by a relative error of at most 0.022.
Values may be sent and summed in bfloat16 or wider, within the bound.
No kernel may reach another device: no remote copies, remote signals or barrier semaphores. Data moves between devices by JAX's collectives and lax.ppermute only.
A program may use at most 64 MiB of HBM per device.

```python
import math
import jax
import jax.numpy as jnp
import numpy as np
from jax import lax

D = 4096
TAPS = 128
TOKENS = 8192
CONTIGS = 64
LONGEST = 768
N_ROW = 32
N_COL = 8


def levels(stream_key, extent, shards, low, high):
    gain, own = 1.0, jax.random.fold_in(stream_key, 6)
    for dim, shards_of in shards:
        heights = jnp.exp(jax.random.uniform(jax.random.fold_in(own, dim), (shards_of,), jnp.float32, low / len(shards), high / len(shards)))
        gain = gain * jnp.repeat(heights, extent[dim] // shards_of).reshape([-1 if axis == dim else 1 for axis in range(len(extent))])
    return gain


def split_up(amount, total, most, slope):
    loads = [(1 << 20) // math.isqrt(rank ** slope) + 1 for rank in range(2, amount + 1)]
    surplus, given = total - most - (amount - 1), [1] * (amount - 1)
    while surplus > 0:
        movable = [i for i in range(amount - 1) if given[i] < most]
        mass, budget = sum([loads[i] for i in movable]), surplus
        for i in movable:
            extra = min(most - given[i], max(1, budget * loads[i] // mass), surplus)
            given[i] = given[i] + extra
            surplus = surplus - extra
    return np.array([most] + given)


def uneven_parts(stream_key, amount, total, limit, lean):
    if amount == 2:
        one = jax.random.randint(stream_key, (), max(1, total - limit), min(limit, total - 1) + 1)
        return jnp.stack([one, total - one])
    lengths = jnp.asarray(split_up(amount, total, limit, lean), jnp.int32)
    twos = (amount - 1) // 2
    donor, taker = lengths[1:1 + 2 * twos:2], lengths[2:2 + 2 * twos:2]
    slack = jnp.minimum(donor - 1, limit - taker)
    moved = jax.random.randint(jax.random.fold_in(stream_key, 1), (twos,), 0, 1 << 20) % (slack + 1)
    lengths = lengths.at[1:1 + 2 * twos:2].set(donor - moved).at[2:2 + 2 * twos:2].set(taker + moved)
    return lengths[jax.random.permutation(jax.random.fold_in(stream_key, 2), amount)]


def normal_values(own_key, shape, deviation, reach, pieces=(), kind=jnp.bfloat16):
    entries = deviation * jax.random.normal(own_key, shape, jnp.float32)
    if pieces:
        entries = entries * levels(own_key, shape, pieces, -0.22, 0.18)
    return jnp.clip(entries, -reach, reach).astype(kind)


def setup_inputs(seed: int = 0) -> dict:
    streams_of = jax.random.split(jax.random.key(seed), 6)
    tokens = normal_values(streams_of[0], (TOKENS, D), 1.0, 6.0, ((0, 32), (1, 8)))
    contig_lengths = uneven_parts(streams_of[1], CONTIGS, TOKENS, LONGEST, 1).astype(jnp.int32)
    w_in = normal_values(streams_of[2], (D, D), D ** -0.5, 0.09375, ((0, 32), (1, 8)))
    conv_filter = normal_values(streams_of[3], (TAPS, D), TAPS ** -0.5, 0.5, ((1, 8),), jnp.float32)
    d_gated = normal_values(streams_of[4], (TOKENS, D), 1.0, 6.0, ((0, 32), (1, 8)))
    return dict(tokens=tokens, contig_lengths=contig_lengths, w_in=w_in, conv_filter=conv_filter, d_gated=d_gated)


def contig_offsets(contig_lengths, positions):
    ends = jnp.cumsum(contig_lengths).astype(jnp.int32)
    starts = ends - contig_lengths
    before = jnp.where(starts[None, :] <= positions[:, None], starts[None, :], 0)
    return positions - lax.optimization_barrier(jnp.max(before, axis=1))

def column_blocks(left, right, count):
    left_parts = jnp.moveaxis(left.reshape(left.shape[0], count, -1), 1, 0)
    right_parts = jnp.moveaxis(right.reshape(right.shape[0], count, -1), 1, 0)

    def add_block(running, pair):
        term = lax.dot_general(pair[0], pair[1], (((1,), (1,)), ((), ())), preferred_element_type=jnp.float32)
        rounded = lax.optimization_barrier(term.astype(jnp.bfloat16))
        return (running + rounded.astype(jnp.float32), None)
    initial = jnp.zeros((left.shape[0], right.shape[0]), jnp.float32)
    result, _ = lax.scan(add_block, initial, (left_parts, right_parts))
    return result

def token_blocks(left, right, count):
    left_parts = left.reshape(count, -1, left.shape[1])
    right_parts = right.reshape(count, -1, right.shape[1])

    def add_block(running, pair):
        term = lax.dot_general(pair[0], pair[1], (((0,), (0,)), ((), ())), preferred_element_type=jnp.float32)
        rounded = lax.optimization_barrier(term.astype(jnp.bfloat16))
        return (running + rounded.astype(jnp.float32), None)
    initial = jnp.zeros((left.shape[1], right.shape[1]), jnp.float32)
    result, _ = lax.scan(add_block, initial, (left_parts, right_parts))
    return result

def reference(tokens, contig_lengths, w_in, conv_filter, d_gated):
    seq_total = tokens.shape[0]
    projected = jnp.dot(tokens, w_in, preferred_element_type=jnp.float32).astype(jnp.bfloat16)
    proj_f = projected.astype(jnp.float32)
    positions = jnp.arange(seq_total, dtype=jnp.int32)
    offsets = contig_offsets(contig_lengths, positions)
    padded = jnp.concatenate([jnp.zeros((TAPS - 1, D), jnp.float32), proj_f], 0)

    def conv_step(tap, running):
        shifted = lax.dynamic_slice_in_dim(padded, (TAPS - 1 - tap).astype(jnp.int32), seq_total, 0)
        weight = lax.dynamic_slice_in_dim(conv_filter, tap.astype(jnp.int32), 1, 0)
        return running + jnp.where((tap <= offsets)[:, None], shifted * weight, 0.0)
    conv_out = lax.fori_loop(jnp.int32(0), jnp.int32(TAPS), conv_step, jnp.zeros((seq_total, D), jnp.float32))
    sigma = jax.nn.sigmoid(proj_f)
    gate_val = proj_f * sigma
    gated = (conv_out * gate_val).astype(jnp.bfloat16)
    upstream = d_gated.astype(jnp.float32)
    d_conv = upstream * gate_val
    d_gate = upstream * conv_out * (sigma * (1.0 + proj_f * (1.0 - sigma)))
    ext_grad = jnp.concatenate([d_conv, jnp.zeros((TAPS - 1, D), jnp.float32)], 0)
    ext_offsets = contig_offsets(contig_lengths, jnp.arange(seq_total + TAPS - 1, dtype=jnp.int32))

    def back_step(tap, running):
        shifted = lax.dynamic_slice_in_dim(ext_grad, tap.astype(jnp.int32), seq_total, 0)
        live = lax.dynamic_slice_in_dim(ext_offsets, tap.astype(jnp.int32), seq_total, 0) >= tap
        weight = lax.dynamic_slice_in_dim(conv_filter, tap.astype(jnp.int32), 1, 0)
        return running + jnp.where(live[:, None], shifted * weight, 0.0)
    back_conv = lax.fori_loop(jnp.int32(0), jnp.int32(TAPS), back_step, jnp.zeros((seq_total, D), jnp.float32))
    d_proj = (back_conv + d_gate).astype(jnp.bfloat16)
    grad_in = token_blocks(tokens, d_proj, N_ROW) / math.sqrt(seq_total)
    d_tokens = column_blocks(d_proj, w_in, N_COL).astype(jnp.bfloat16)
    return (gated, d_tokens, grad_in)
```

```python
import functools
import math

import jax
import jax.numpy as jnp
from jax import lax
from jax.experimental import pallas as pl
from jax.experimental.pallas import tpu as pltpu
from jax.sharding import PartitionSpec as P

BF = jnp.bfloat16
F32 = jnp.float32
NY, NX, NC, NZ = 4, 4, 2, 8
TILE = 16
LANES = 128


def around_z(value, steps):
    return lax.ppermute(value, "col", [(z, (z + steps) % NZ) for z in range(NZ)])


def around_row(value, dy=0, dx=0, dc=0):
    pairs = []
    for y in range(NY):
        for x in range(NX):
            for c in range(NC):
                to = (((y + dy) % NY) * NX + (x + dx) % NX) * NC + (c + dc) % NC
                pairs.append(((y * NX + x) * NC + c, to))
    return lax.ppermute(value, "row", pairs)


def next_row(value, steps):
    count = NY * NX * NC
    return lax.ppermute(value, "row", [(r, (r + steps) % count) for r in range(count)])


def live_taps(contig_lengths, first_row, rows):
    ends = jnp.cumsum(contig_lengths)
    starts = ends - contig_lengths
    at = first_row + jnp.arange(rows, dtype=jnp.int32)
    start = jnp.max(jnp.where(starts[None, :] <= at[:, None], starts[None, :], 0), axis=1)
    end = jnp.min(jnp.where(ends[None, :] > at[:, None], ends[None, :], 1 << 30), axis=1)
    back = jnp.minimum(at - start, 127)
    ahead = jnp.minimum(end - 1 - at, 127)
    wide = lambda v: jnp.broadcast_to(v.astype(BF)[:, None], (rows, LANES))
    return wide(back), wide(ahead)


def gather_tokens(t):
    half = t.shape[0] // 2
    r1, l1 = around_z(t, 1), around_z(t, -1)
    r2, l2 = around_z(r1, 1), around_z(l1, -1)
    r3, l3 = around_z(r2, 1), around_z(l2, -1)
    r4, l4 = around_z(r3[:half], 1), around_z(l3[half:], -1)
    return [t, l1, l2, l3, r3, r2, r1, r4, l4]


def place(own, others, index):
    buf = jnp.zeros((4,) + own.shape, own.dtype)
    for steps, piece in [(0, own)] + others:
        buf = lax.dynamic_update_index_in_dim(buf, piece, (index + steps) % 4, 0)
    return buf


def spread(own, index, send):
    cut = own.shape[0] // 2
    up, down = send(own, 1), send(own, -1)
    far_up, far_down = send(up[cut:], 1), send(down[:cut], -1)
    far = jnp.concatenate([far_down, far_up], 0)
    return place(own, [(3, up), (1, down), (2, far)], index)


def gather_weight(w, y, x):
    along_x = lambda v, s: around_row(v, dx=s)
    along_y = lambda v, s: around_row(v, dy=s)
    cut = w.shape[1] // 2
    a = spread(spread(w[:, :cut], x, along_x), y, along_y)
    b = spread(spread(w[:, cut:], y, along_y), x, along_x)
    return a, b, around_row(a, dc=1), around_row(b, dc=1)


def build_block(me, a_own, b_own, a_oth, b_oth, w_scr):
    for xp in range(2):
        for own, a_ref, b_ref in ((True, a_own, b_own), (False, a_oth, b_oth)):
            core = me if own else 1 - me
            rows = pl.ds(pl.multiple_of(xp * 256 + core * 128, 128), 128)
            w_scr[rows, 0:256] = a_ref[0, xp]
            w_scr[rows, 256:512] = b_ref[xp, 0]


def project_kernel(
    ids, t0, l1, l2, l3, r3, r2, r1, r4, l4, a_own, b_own, a_oth, b_oth, dg_ref,
    p_ref, head_ref, mine_ref, cross_ref, acc, w_scr, t_scr,
):
    step = pl.program_id(0)
    me = ids[2]
    build_block(me, a_own, b_own, a_oth, b_oth, w_scr)

    def take(piece):
        t_scr[...] = piece[...]

    for at, piece in enumerate((t0, l1, l2, l3, None, r3, r2, r1)):
        if piece is None:

            @pl.when(step == at)
            def _():
                t_scr[0:128] = r4[...]
                t_scr[128:256] = l4[...]
        else:
            pl.when(step == at)(functools.partial(take, piece))

    for xp in range(2):
        mine = pl.ds(pl.multiple_of(xp * 256 + me * 128, 128), 128)
        cross = pl.ds(pl.multiple_of(xp * 256 + (1 - me) * 128, 128), 128)
        mine_ref[0, :, xp * 128 : xp * 128 + 128] = t_scr[:, mine]
        cross_ref[0, :, xp * 128 : xp * 128 + 128] = t_scr[:, cross]

    term = jnp.dot(t_scr[...], w_scr[...], preferred_element_type=F32)

    @pl.when(step == 0)
    def _():
        acc[...] = term

    @pl.when(step > 0)
    def _():
        acc[...] += term

    @pl.when(step == NZ - 1)
    def _():
        p = acc[...].astype(BF)
        p_ref[...] = p
        top = p[0:128].astype(F32)
        up = dg_ref[...].astype(F32)
        head_ref[...] = (up * (top * jax.nn.sigmoid(top))).astype(BF)


def weight_specs(block):
    a = pl.BlockSpec((1, 2, 128, 256), lambda s, ids: (block(s, ids) // 2, block(s, ids) % 2, 0, 0))
    b = pl.BlockSpec((2, 1, 128, 256), lambda s, ids: (block(s, ids) % 2, block(s, ids) // 2, 0, 0))
    return [a, b, a, b]


def project(ids, pieces, weight, d_gated):
    whole = lambda v: pl.BlockSpec(v.shape, lambda s, ids: (0,) * v.ndim)
    block = lambda s, ids: lax.rem(ids[3] + s, NZ)
    tok = pl.BlockSpec((1, 256, 256), lambda s, ids: (block(s, ids), 0, 0))
    fixed = lambda shape: pl.BlockSpec(shape, lambda s, ids: (0, 0))
    return pl.pallas_call(
        project_kernel,
        grid_spec=pltpu.PrefetchScalarGridSpec(
            num_scalar_prefetch=1,
            grid=(NZ,),
            in_specs=[whole(v) for v in pieces] + weight_specs(block) + [fixed((128, 512))],
            out_specs=[fixed((256, 512)), fixed((128, 512)), tok, tok],
            scratch_shapes=[
                pltpu.VMEM((256, 512), F32),
                pltpu.VMEM((512, 512), BF),
                pltpu.VMEM((256, 512), BF),
            ],
        ),
        out_shape=[
            jax.ShapeDtypeStruct((256, 512), BF),
            jax.ShapeDtypeStruct((128, 512), BF),
            jax.ShapeDtypeStruct((NZ, 256, 256), BF),
            jax.ShapeDtypeStruct((NZ, 256, 256), BF),
        ],
        compiler_params=pltpu.CompilerParams(vmem_limit_bytes=24 << 20),
        cost_estimate=pl.CostEstimate(flops=2 * 256 * 4096 * 512, bytes_accessed=8 << 20, transcendentals=0),
        name="project",
    )(ids, *pieces, *weight, d_gated)


def mix(ext, tile_of, live_ref, taps_ref, lanes, acc, reverse):
    rows = ext.shape[0]
    acc[...] = jnp.zeros_like(acc)
    for b in range(TILE):
        shift = (rows - b) % rows if reverse else b
        moved = (pltpu.roll(ext, shift, 0) if shift else ext).astype(BF)
        weights = [
            jnp.broadcast_to(taps_ref[TILE * a + b : TILE * a + b + 1, lanes], (TILE, LANES)).astype(BF)
            for a in range(8)
        ]
        for u in range(16):
            live = live_ref[TILE * u : TILE * u + TILE, :]
            total = None
            for a in range(8):
                at = TILE * tile_of(u, a)
                term = jnp.where(live >= TILE * a + b, moved[at : at + TILE] * weights[a], jnp.zeros((), BF))
                total = term if total is None else total + term
            acc[TILE * u : TILE * u + TILE, :] += total.astype(F32)


def conv_kernel(p_ref, tail_ref, head_ref, dg_ref, taps_ref, back_ref, ahead_ref, gated_ref, dproj_ref, ext, acc):
    def strip(s, carry):
        lanes = pl.ds(pl.multiple_of(s * LANES, LANES), LANES)
        p = p_ref[:, lanes].astype(F32)
        ext[0:128] = tail_ref[:, lanes].astype(F32)
        ext[128:384] = p
        mix(ext[...], lambda u, a: u + 8 - a, back_ref, taps_ref, lanes, acc, False)
        conv = acc[...]
        sigma = jax.nn.sigmoid(p)
        gate = p * sigma
        gated_ref[:, lanes] = (conv * gate).astype(BF)
        up = dg_ref[:, lanes].astype(F32)
        d_gate = up * conv * (sigma * (1.0 + p * (1.0 - sigma)))
        ext[0:256] = up * gate
        ext[256:384] = head_ref[:, lanes].astype(F32)
        mix(ext[...], lambda u, a: u + a, ahead_ref, taps_ref, lanes, acc, True)
        dproj_ref[:, lanes] = (acc[...] + d_gate).astype(BF)
        return carry

    lax.fori_loop(jnp.int32(0), jnp.int32(4), strip, jnp.int32(0))


def conv(p, tail, head, d_gated, taps, back, ahead):
    return pl.pallas_call(
        conv_kernel,
        out_shape=[jax.ShapeDtypeStruct((256, 512), BF)] * 2,
        scratch_shapes=[pltpu.VMEM((384, LANES), F32), pltpu.VMEM((256, LANES), F32)],
        compiler_params=pltpu.CompilerParams(vmem_limit_bytes=24 << 20),
        cost_estimate=pl.CostEstimate(flops=8 * 256 * 512 * 128, bytes_accessed=2 << 20, transcendentals=0),
        name="conv",
    )(p, tail, head, d_gated, taps, back, ahead)


def back_kernel(order, ids, d_ref, a_own, b_own, a_oth, b_oth, *refs):
    outs, w_scr = refs[:-1], refs[-1]
    build_block(ids[2], a_own, b_own, a_oth, b_oth, w_scr)
    term = lax.dot_general(d_ref[...], w_scr[...], (((1,), (1,)), ((), ())), preferred_element_type=F32)
    term = term.astype(BF)
    for at in range(len(order)):

        @pl.when(pl.program_id(0) == at)
        def _(at=at):
            outs[at][...] = term


def token_terms(ids, d_proj, weight, order):
    def block(s, ids):
        steps = jnp.int32(order[0])
        for at in range(1, len(order)):
            steps = jnp.where(s == at, jnp.int32(order[at]), steps)
        return lax.rem(ids[3] + steps, NZ)

    fixed = pl.BlockSpec((256, 512), lambda s, ids: (0, 0))
    return pl.pallas_call(
        functools.partial(back_kernel, order),
        grid_spec=pltpu.PrefetchScalarGridSpec(
            num_scalar_prefetch=1,
            grid=(len(order),),
            in_specs=[fixed] + weight_specs(block),
            out_specs=[fixed] * len(order),
            scratch_shapes=[pltpu.VMEM((512, 512), BF)],
        ),
        out_shape=[jax.ShapeDtypeStruct((256, 512), BF)] * len(order),
        compiler_params=pltpu.CompilerParams(vmem_limit_bytes=24 << 20),
        cost_estimate=pl.CostEstimate(
            flops=2 * 256 * 512 * 512 * len(order), bytes_accessed=len(order) << 20, transcendentals=0
        ),
        name="token_terms",
    )(ids, d_proj, *weight)


def add(u, v):
    return (u.astype(F32) + v.astype(F32)).astype(BF)


def sum_tokens(near, far):
    r3, l3, r2, l2, r1, l1, own = near
    half = far.shape[0] // 2
    r, l = around_z(far[:half], 1), around_z(far[half:], -1)
    r = around_z(jnp.concatenate([add(r3[:half], r), r3[half:]], 0), 1)
    l = around_z(jnp.concatenate([l3[:half], add(l3[half:], l)], 0), -1)
    r, l = around_z(add(r2, r), 1), around_z(add(l2, l), -1)
    r, l = around_z(add(r1, r), 1), around_z(add(l1, l), -1)
    return (own.astype(F32) + r.astype(F32) + l.astype(F32)).astype(BF)


def grad_kernel(ids, mine_ref, theirs_ref, d_mine, d_theirs, ga_ref, gb_ref):
    def one(zb, carry):
        dims = (((0,), (0,)), ((), ()))
        total = lax.dot_general(mine_ref[zb], d_mine[...], dims, preferred_element_type=F32)
        total += lax.dot_general(theirs_ref[zb], d_theirs[...], dims, preferred_element_type=F32)
        total = total.astype(BF)
        ky = lax.rem(zb // 2 + NY - ids[0], NY)
        for xp in range(2):
            kx = lax.rem(lax.rem(zb, 2) * 2 + xp + NX - ids[1], NX)
            ga_ref[ky, kx] = total[xp * 128 : xp * 128 + 128, 0:256]
            gb_ref[kx, ky] = total[xp * 128 : xp * 128 + 128, 256:512]
        return carry

    lax.fori_loop(jnp.int32(0), jnp.int32(NZ), one, jnp.int32(0))


def weight_terms(ids, mine, theirs, d_mine, d_theirs):
    vmem = pl.BlockSpec(memory_space=pltpu.VMEM)
    return pl.pallas_call(
        grad_kernel,
        in_specs=[pl.BlockSpec(memory_space=pltpu.SMEM)] + [vmem] * 4,
        out_specs=[vmem, vmem],
        out_shape=[jax.ShapeDtypeStruct((4, 4, 128, 256), BF)] * 2,
        compiler_params=pltpu.CompilerParams(vmem_limit_bytes=24 << 20),
        cost_estimate=pl.CostEstimate(flops=2 * 512 * 2048 * 512, bytes_accessed=5 << 20, transcendentals=0),
        name="weight_terms",
    )(ids, mine, theirs, d_mine, d_theirs)


def sum_axis(blocks, send):
    cut = blocks[2].shape[0] // 2
    up, down = send(blocks[2][:cut], 1), send(blocks[2][cut:], -1)
    up = send(jnp.concatenate([add(blocks[1][:cut], up), blocks[1][cut:]], 0), 1)
    down = send(jnp.concatenate([blocks[3][:cut], add(blocks[3][cut:], down)], 0), -1)
    return blocks[0].astype(F32) + up.astype(F32) + down.astype(F32)


def sum_weight(ga, gb):
    along_x = lambda v, s: around_row(v, dx=s)
    along_y = lambda v, s: around_row(v, dy=s)
    a = sum_axis([ga[k] for k in range(4)], along_y).astype(BF)
    b = sum_axis([gb[k] for k in range(4)], along_x).astype(BF)
    a = sum_axis([a[k] for k in range(4)], along_x)
    b = sum_axis([b[k] for k in range(4)], along_y)
    return jnp.concatenate([a, b], 1)


def body(tokens, contig_lengths, w_in, conv_filter, d_gated):
    rows = tokens.shape[0]
    seq_total = rows * NY * NX * NC
    row, z = lax.axis_index("row"), lax.axis_index("col")
    core, chip = row % NC, row // NC
    y, x = chip // NX, chip % NX
    ids = jnp.stack([y, x, core, z]).astype(jnp.int32)

    pieces = gather_tokens(tokens)
    weight = gather_weight(w_in, y, x)
    back, ahead = live_taps(contig_lengths, row * rows, rows)
    projected, head, mine, cross = project(ids, pieces, weight, d_gated)
    tail = next_row(projected[rows - 128 :], 1)
    next_head = next_row(head, -1)
    theirs = around_row(cross, dc=1)
    gated, d_proj = conv(projected, tail, next_head, d_gated, conv_filter, back, ahead)
    (far,) = token_terms(ids, d_proj, weight, [4])
    near = token_terms(ids, d_proj, weight, [3, 5, 2, 6, 1, 7, 0])
    d_tokens = sum_tokens(near, far)
    d_theirs = around_row(d_proj, dc=1)
    ga, gb = weight_terms(ids, mine, theirs, d_proj, d_theirs)
    grad_in = sum_weight(ga, gb) * (1.0 / math.sqrt(seq_total))
    return gated, d_tokens, grad_in


def solution(mesh):
    placed = (P("row", "col"), P(), P("row", "col"), P(None, "col"), P("row", "col"))
    return jax.shard_map(
        body,
        mesh=mesh,
        in_specs=placed,
        out_specs=(P("row", "col"), P("row", "col"), P("row", "col")),
        check_vma=False,
    )
```

```python
import functools
import math

import jax
import jax.numpy as jnp
from jax import lax
from jax.experimental import pallas as pl
from jax.experimental.pallas import tpu as pltpu
from jax.sharding import PartitionSpec as P

BF = jnp.bfloat16
F32 = jnp.float32
NY, NX, NC, NZ = 4, 4, 2, 8
TILE = 16
LANES = 128


def row_of(y, x, c):
    return ((y % NY) * NX + x % NX) * NC + c % NC


CHIPS = [(y, x) for y in range(NY) for x in range(NX)]
def around_z(value, steps):
    pairs = []
    for y, x in CHIPS:
        for c in range(NC):
            for z in range(NZ):
                to = (z + steps * (1 - 2 * c)) % NZ
                pairs.append((row_of(y, x, c) * NZ + z, row_of(y, x, c) * NZ + to))
    return lax.ppermute(value, ("row", "col"), pairs)


def narrow(value, steps):
    pairs = []
    for y, x in CHIPS:
        pairs.append((row_of(y, x, 0), row_of(y, x + steps, 0)))
        pairs.append((row_of(y, x, 1), row_of(y + steps, x, 1)))
    return lax.ppermute(value, "row", pairs)


def wide(value, steps):
    pairs = []
    for y, x in CHIPS:
        pairs.append((row_of(y, x, 0), row_of(y + steps, x, 0)))
        pairs.append((row_of(y, x, 1), row_of(y, x + steps, 1)))
    return lax.ppermute(value, "row", pairs)


def to_other_core(value):
    return lax.ppermute(value, "row", [(row_of(y, x, c), row_of(y, x, c + 1)) for y, x in CHIPS for c in range(NC)])


def next_row(value, steps):
    count = NY * NX * NC
    return lax.ppermute(value, "row", [(r, (r + steps) % count) for r in range(count)])


def live_taps(contig_lengths, first_row, rows):
    ends = jnp.cumsum(contig_lengths)
    starts = ends - contig_lengths
    at = first_row + jnp.arange(rows, dtype=jnp.int32)
    start = jnp.max(jnp.where(starts[None, :] <= at[:, None], starts[None, :], 0), axis=1)
    end = jnp.min(jnp.where(ends[None, :] > at[:, None], ends[None, :], 1 << 30), axis=1)
    back = jnp.minimum(at - start, 127)
    ahead = jnp.minimum(end - 1 - at, 127)
    wide = lambda v: jnp.broadcast_to(v.astype(BF)[:, None], (rows, LANES))
    return wide(back), wide(ahead)


def after(value, *others):
    return lax.optimization_barrier((value, others))[0]


VMEM = pl.BlockSpec(memory_space=pltpu.VMEM)
SMEM = pl.BlockSpec(memory_space=pltpu.SMEM)
HBM = pl.BlockSpec(memory_space=pltpu.HBM)


def loop(count, step):
    def run(i, carry):
        step(i)
        return carry

    lax.fori_loop(jnp.int32(0), jnp.int32(count), run, jnp.int32(0))


def add_kernel(a, b, out):
    out[...] = (a[...].astype(F32) + b[...].astype(F32)).astype(BF)


def add(a, b):
    return pl.pallas_call(
        add_kernel,
        in_specs=[VMEM] * 2,
        out_specs=VMEM,
        out_shape=jax.ShapeDtypeStruct(a.shape, BF),
        compiler_params=pltpu.CompilerParams(vmem_limit_bytes=2 << 20),
        cost_estimate=pl.CostEstimate(flops=1 << 20, bytes_accessed=1 << 20, transcendentals=0),
        name="add",
    )(a, b)


def stack_kernel(first, *refs):
    for k in range(4):
        refs[4][lax.rem(first[0] + k, 4)] = refs[k][...]


def stack(first, pieces):
    return pl.pallas_call(
        stack_kernel,
        in_specs=[SMEM] + [VMEM] * 4,
        out_specs=VMEM,
        out_shape=jax.ShapeDtypeStruct((4, 128, 512), BF),
        compiler_params=pltpu.CompilerParams(vmem_limit_bytes=2 << 20),
        cost_estimate=pl.CostEstimate(flops=1 << 20, bytes_accessed=1 << 20, transcendentals=0),
        name="stack",
    )(first, *pieces)


def sum_kernel(*refs):
    for j in range(4):
        total = refs[0][j].astype(F32)
        for k in range(1, 4):
            total += refs[k][j].astype(F32)
        refs[4 + j][...] = total.astype(BF)


def sum_four(blocks):
    return pl.pallas_call(
        sum_kernel,
        in_specs=[VMEM] * 4,
        out_specs=[VMEM] * 4,
        out_shape=[jax.ShapeDtypeStruct((128, 512), BF)] * 4,
        compiler_params=pltpu.CompilerParams(vmem_limit_bytes=4 << 20),
        cost_estimate=pl.CostEstimate(flops=1 << 20, bytes_accessed=1 << 20, transcendentals=0),
        name="sum_four",
    )(*blocks)


def place_of(ids, steps):
    return lax.rem(ids[3] + jnp.where(ids[2] == 0, steps, NZ - steps), NZ)


def load_weight(ids, own, other, w, sems, act):
    def one_core(core, blocks, base):
        for i, block in enumerate(blocks):
            if core == 0:
                y = lax.rem(ids[0] + i, 4)
                for half in range(2):
                    at = w.at[2 * y + half, :, 0]
                    act(pltpu.make_async_copy(block.at[2 * half : 2 * half + 2], at, sems.at[base + 2 * i + half]))
            else:
                x = lax.rem(ids[1] + i, 4)
                for y in range(4):
                    at = w.at[2 * y + x // 2, lax.rem(x, 2), 1]
                    act(pltpu.make_async_copy(block.at[y], at, sems.at[base + 4 * i + y]))

    @pl.when(ids[2] == 0)
    def _():
        one_core(0, own, 0)
        one_core(1, other, 8)

    @pl.when(ids[2] == 1)
    def _():
        one_core(0, other, 0)
        one_core(1, own, 8)


def start(copy):
    copy.start()


def wait(copy):
    copy.wait()


def start(copy):
    copy.start()


def wait(copy):
    copy.wait()


def project_piece(ids, k, piece, w, mine_ref, cross_ref):
    for core, out in ((ids[2], mine_ref), (1 - ids[2], cross_ref)):
        for xp in range(2):
            lanes = pl.ds(pl.multiple_of(xp * 256 + core * 128, 128), 128)
            out[k, :, xp * 128 : xp * 128 + 128] = piece[:, lanes]
    return jnp.dot(piece[...], w[place_of(ids, k)].reshape(512, 512), preferred_element_type=F32)


EARLY, LATE = (0, 1, 7, 2, 6), (3, 5, 4)


def early_kernel(ids, *refs):
    pieces, own, other, (acc, w, mine_ref, cross_ref, tok, sems, tok_sems) = refs[0:5], refs[5:9], refs[9:13], refs[13:]
    load_weight(ids, own, other, w, sems, start)
    arrive = [pltpu.make_async_copy(piece, tok.at[n], tok_sems.at[n]) for n, piece in enumerate(pieces)]
    for copy in arrive:
        copy.start()
    load_weight(ids, own, other, w, sems, wait)
    total = None
    for n, k in enumerate(EARLY):
        arrive[n].wait()
        term = project_piece(ids, k, tok.at[n], w, mine_ref, cross_ref)
        total = term if total is None else total + term
    acc[...] = total


def late_kernel(ids, *refs):
    pieces, (acc, w, _, _, dg_ref, p_ref, tail_ref, head_ref, mine_ref, cross_ref) = refs[0:3], refs[3:]
    total = acc[...]
    for k, piece in zip(LATE, pieces):
        total += project_piece(ids, k, piece, w, mine_ref, cross_ref)
    p = total.astype(BF)
    p_ref[...] = p
    tail_ref[...] = p[128:256]
    top = p[0:128].astype(F32)
    head_ref[...] = (dg_ref[0:128].astype(F32) * (top * jax.nn.sigmoid(top))).astype(BF)


def project_early(ids, pieces, blocks):
    part_of = jax.ShapeDtypeStruct((NZ, 256, 256), BF)
    return pl.pallas_call(
        early_kernel,
        in_specs=[SMEM] + [HBM] * 13,
        out_specs=[VMEM] * 4,
        out_shape=[
            jax.ShapeDtypeStruct((256, 512), F32), jax.ShapeDtypeStruct((NZ, 2, 2, 128, 512), BF), part_of, part_of,
        ],
        scratch_shapes=[
            pltpu.VMEM((5, 256, 512), BF),
            pltpu.SemaphoreType.DMA((24,)),
            pltpu.SemaphoreType.DMA((5,)),
        ],
        compiler_params=pltpu.CompilerParams(vmem_limit_bytes=8 << 20),
        cost_estimate=pl.CostEstimate(flops=1 << 32, bytes_accessed=8 << 20, transcendentals=0),
        name="project_early",
    )(ids, *pieces, *blocks)


def project_late(ids, pieces, early, d_gated):
    half, part_of = jax.ShapeDtypeStruct((128, 512), BF), jax.ShapeDtypeStruct((NZ, 256, 256), BF)
    return pl.pallas_call(
        late_kernel,
        in_specs=[SMEM] + [VMEM] * 8,
        out_specs=[VMEM] * 5,
        out_shape=[jax.ShapeDtypeStruct((256, 512), BF), half, half, part_of, part_of],
        input_output_aliases={6: 3, 7: 4},
        compiler_params=pltpu.CompilerParams(vmem_limit_bytes=6 << 20),
        cost_estimate=pl.CostEstimate(flops=2 * 256 * 1536 * 512, bytes_accessed=4 << 20, transcendentals=0),
        name="project_late",
    )(ids, *pieces, *early, d_gated)


def mix(ext, live_ref, taps_ref, even, odd, mask, acc, reverse):
    acc[...] = jnp.zeros_like(acc)
    rows = ext.shape[0]

    def shift(b):
        for k in range(16):
            limit = (b + (8 * k - 1)).astype(F32).astype(BF)
            for u in range(8):
                at = slice(TILE * u, TILE * u + TILE)
                mask[k, at] = jnp.clip(live_ref[at] - limit, jnp.zeros((), BF), jnp.ones((), BF))

        def strip(s):
            lanes = pl.ds(pl.multiple_of(s * 256, 256), 256)
            if reverse:
                r = pltpu.roll(ext[:, lanes], lax.rem(rows - b, rows), 0)
                even[...] = r.astype(BF)
                odd[...] = jnp.concatenate([r[8:], r[:8]], 0).astype(BF)
            else:
                r = pltpu.roll(ext[:, lanes], b, 0)
                even[...] = r.astype(BF)
                odd[...] = jnp.concatenate([r[-8:], r[:-8]], 0).astype(BF)
            for h, moved in ((0, even), (1, odd)):
                weights = [taps_ref[b, 2 * a + h, :, lanes] for a in range(8)]
                sums = [None] * 8
                count = [0] * 8
                for v in range(16):
                    source = moved[TILE * v : TILE * v + TILE]
                    for a in range(8):
                        u = v - a if reverse else v - 8 + a
                        if not 0 <= u < 8:
                            continue
                        at = slice(TILE * u, TILE * u + TILE)
                        m = mask[2 * a + h, at]
                        term = source * weights[a] * jnp.concatenate([m, m], 1)
                        sums[u] = term if sums[u] is None else sums[u] + term
                        count[u] += 1
                        if count[u] == 8:
                            acc[at, lanes] += sums[u].astype(F32)

        loop(2, strip)

    loop(8, shift)


def gates(p, up, out):
    sigma = jax.nn.sigmoid(p)
    gate = p * sigma
    return (out * gate).astype(BF), up * out * (sigma * (1.0 + p * (1.0 - sigma))), up * gate


LOW, HIGH = slice(0, 128), slice(128, 256)


def ahead_inside_kernel(p_ref, dg_ref, taps_ref, live_ref, gated_ref, dgate_ref, ext, even, odd, mask, acc):
    ext[...] = p_ref[...].astype(F32)
    mix(ext, live_ref.at[HIGH], taps_ref, even, odd, mask, acc, False)
    p, up = p_ref[HIGH].astype(F32), dg_ref[HIGH].astype(F32)
    gated_ref[...], dgate_ref[...], _ = gates(p, up, acc[...])


def back_inside_kernel(p_ref, dg_ref, taps_ref, live_ref, part_ref, dconv_ref, ext, even, odd, mask, acc):
    p = p_ref[...].astype(F32)
    ext[...] = dg_ref[...].astype(F32) * (p * jax.nn.sigmoid(p))
    dconv_ref[...] = ext[HIGH]
    mix(ext, live_ref.at[LOW], taps_ref, even, odd, mask, acc, True)
    part_ref[...] = acc[...]


def ahead_edge_kernel(p_ref, dg_ref, taps_ref, live_ref, tail_ref, gated_hi, part_ref, gated_ref, low_ref, ext, even, odd, mask, acc):
    p, up = p_ref[LOW].astype(F32), dg_ref[LOW].astype(F32)
    ext[LOW] = tail_ref[...].astype(F32)
    ext[HIGH] = p
    mix(ext, live_ref.at[LOW], taps_ref, even, odd, mask, acc, False)
    gated_ref[LOW], d_gate, _ = gates(p, up, acc[...])
    gated_ref[HIGH] = gated_hi[...]
    low_ref[...] = (part_ref[...] + d_gate).astype(BF)


def back_edge_kernel(
    dconv_ref, head_ref, taps_ref, live_ref, low_ref, dgate_ref, ids, w_ref, dproj_ref, far_ref, w,
    ext, even, odd, mask, acc, sem,
):
    load = pltpu.make_async_copy(w_ref, w, sem)
    load.start()
    ext[LOW] = dconv_ref[...]
    ext[HIGH] = head_ref[...].astype(F32)
    mix(ext, live_ref.at[HIGH], taps_ref, even, odd, mask, acc, True)
    dproj_ref[LOW] = low_ref[...]
    dproj_ref[HIGH] = (acc[...] + dgate_ref[...]).astype(BF)
    load.wait()
    far_ref[...] = back_term(dproj_ref[...], w[place_of(ids, 4)].reshape(512, 512))


def back_term(d, block):
    return lax.dot_general(d, block, (((1,), (1,)), ((), ())), preferred_element_type=F32).astype(BF)


def mix_call(kernel, name, shapes, *operands, specs=None, scratch=()):
    return pl.pallas_call(
        kernel,
        in_specs=specs or [VMEM] * len(operands),
        out_specs=[VMEM] * len(shapes),
        out_shape=[jax.ShapeDtypeStruct(shape, kind) for shape, kind in shapes],
        scratch_shapes=[
            pltpu.VMEM((256, 512), F32),
            pltpu.VMEM((256, 256), BF),
            pltpu.VMEM((256, 256), BF),
            pltpu.VMEM((16, 128, LANES), BF),
            pltpu.VMEM((128, 512), F32),
            *scratch,
        ],
        compiler_params=pltpu.CompilerParams(vmem_limit_bytes=8 << 20),
        cost_estimate=pl.CostEstimate(flops=1 << 32, bytes_accessed=4 << 20, transcendentals=0),
        name=name,
    )(*operands)


def conv(ids, p, tail, head, d_gated, taps, back, ahead, w, cross):
    half, whole = (128, 512), (256, 512)
    tail = next_row(tail, 1)
    gated_hi, dgate_hi = mix_call(
        ahead_inside_kernel, "ahead_inside", [(half, BF), (half, F32)], p, d_gated, taps, back
    )
    head = next_row(after(head, gated_hi), -1)
    part, dconv_hi = mix_call(
        back_inside_kernel, "back_inside", [(half, F32), (half, F32)], p, d_gated, taps, ahead
    )
    theirs = to_other_core(after(cross, part))
    gated, low = mix_call(
        ahead_edge_kernel, "ahead_edge", [(whole, BF), (half, BF)], p, d_gated, taps, back, tail, gated_hi, part
    )
    d_proj, far, w = mix_call(
        back_edge_kernel, "back_edge", [(whole, BF), (whole, BF), (w.shape, BF)],
        dconv_hi, head, taps, ahead, low, dgate_hi, ids, w,
        specs=[VMEM] * 6 + [SMEM, HBM], scratch=[pltpu.SemaphoreType.DMA],
    )
    return gated, d_proj, far, w, theirs


NEAR = (3, 5, 2, 6, 1, 7, 0)


def near_kernel(ids, d_ref, w, *outs):
    d = d_ref[...]
    for steps, out in zip(NEAR, outs):
        out[...] = back_term(d, w[place_of(ids, steps)].reshape(512, 512))


def near_terms(ids, d_proj, weight):
    return pl.pallas_call(
        near_kernel,
        in_specs=[SMEM, VMEM, VMEM],
        out_specs=[VMEM] * 7,
        out_shape=[jax.ShapeDtypeStruct((256, 512), BF)] * 7,
        compiler_params=pltpu.CompilerParams(vmem_limit_bytes=4 << 20),
        cost_estimate=pl.CostEstimate(flops=2 * 256 * 512 * 512 * 7, bytes_accessed=6 << 20, transcendentals=0),
        name="near_terms",
    )(ids, d_proj, weight)


def add_three_kernel(a, b, c, out):
    out[...] = (a[...].astype(F32) + b[...].astype(F32) + c[...].astype(F32)).astype(BF)


def add_three(a, b, c):
    return pl.pallas_call(
        add_three_kernel,
        in_specs=[VMEM] * 3,
        out_specs=VMEM,
        out_shape=jax.ShapeDtypeStruct(a.shape, BF),
        compiler_params=pltpu.CompilerParams(vmem_limit_bytes=2 << 20),
        cost_estimate=pl.CostEstimate(flops=1 << 32, bytes_accessed=1 << 20, transcendentals=0),
        name="add_three",
    )(a, b, c)


def grad_kernel(ids, mine, theirs, d_mine, d_theirs, *refs):
    outs, out = refs[:4], refs[4]
    me = ids[2]
    dims = (((0,), (0,)), ((), ()))
    for k in range(NZ):
        zb = place_of(ids, k)
        total = lax.dot_general(mine[k], d_mine[...], dims, preferred_element_type=F32)
        total += lax.dot_general(theirs[(NZ - k) % NZ], d_theirs[...], dims, preferred_element_type=F32)
        total = total.astype(BF)
        for xp in range(2):
            dy = lax.rem(zb // 2 + 4 - ids[0], 4)
            dx = lax.rem(lax.rem(zb, 2) * 2 + xp + 4 - ids[1], 4)
            out[jnp.where(me == 0, dy, dx), jnp.where(me == 0, dx, dy)] = total[xp * 128 : xp * 128 + 128]
    for k in range(4):
        outs[k][...] = out[k]


def weight_terms(ids, mine, theirs, d_mine, d_theirs):
    return pl.pallas_call(
        grad_kernel,
        in_specs=[SMEM] + [VMEM] * 4,
        out_specs=[VMEM] * 4,
        out_shape=[jax.ShapeDtypeStruct((4, 128, 512), BF)] * 4,
        scratch_shapes=[pltpu.VMEM((4, 4, 128, 512), BF)],
        compiler_params=pltpu.CompilerParams(vmem_limit_bytes=6 << 20),
        cost_estimate=pl.CostEstimate(flops=2 * 512 * 2048 * 512, bytes_accessed=5 << 20, transcendentals=0),
        name="weight_terms",
    )(ids, mine, theirs, d_mine, d_theirs)


def sum_up(ids, d_proj, far, weight, mine, theirs):
    p = around_z(far, 1)
    d_theirs = to_other_core(d_proj)
    p3, q3, p2, q2, p1, q1, own = near_terms(ids, d_proj, weight)
    q = around_z(q3, -1)
    g = weight_terms(ids, mine, theirs, d_proj, after(d_theirs, own))
    p = around_z(add(after(p3, g[0]), p), 1)
    s = [g[0]] + [wide(g[k], k) for k in (1, 2, 3)]
    q = around_z(add(q2, q), -1)
    p = around_z(add(p2, p), 1)
    q_last = add(q1, q)
    q = around_z(q_last, -1)
    p_last = add(p1, p)
    p = around_z(p_last, 1)
    n = sum_four([after(s[0], p_last, q_last)] + s[1:])
    n = [n[0]] + [narrow(n[k], k) for k in (1, 2, 3)]
    d_tokens = add_three(own, p, q)
    return d_tokens, sum(v.astype(F32) for v in n)


def body(tokens, contig_lengths, w_in, conv_filter, d_gated):
    rows = tokens.shape[0]
    seq_total = rows * NY * NX * NC
    row, z = lax.axis_index("row"), lax.axis_index("col")
    core, chip = row % NC, row // NC
    y, x = chip // NX, chip % NX
    ids = jnp.stack([y, x, core, z]).astype(jnp.int32)

    w = [narrow(w_in, 4 - k) for k in (1, 2, 3)]
    p1, q1 = around_z(tokens, 1), around_z(tokens, -1)
    first = jnp.where(core == 0, x, y).astype(jnp.int32).reshape(1)
    row_block = stack(first, [w_in] + w)
    own = [row_block] + [wide(row_block, 4 - k) for k in (1, 2, 3)]
    other = [to_other_core(block) for block in own]
    p2, q2 = around_z(after(p1, row_block), 1), around_z(after(q1, row_block), -1)
    conv_filter, contig_lengths = after((conv_filter, contig_lengths), q1)
    back, ahead = live_taps(contig_lengths, row * rows, rows)
    taps = conv_filter.astype(BF).reshape(16, 8, 1, 512).transpose(1, 0, 2, 3)
    taps = jnp.broadcast_to(taps, (8, 16, TILE, 512))
    p3, q3 = around_z(p2, 1), around_z(q2, -1)
    p4 = around_z(after(p3, back, ahead, taps), 1)
    early = project_early(ids, [tokens, q1, p1, q2, p2], own + other)
    weight = early[1]
    projected, tail, head, mine, cross = project_late(ids, [q3, p3, p4], early, d_gated)
    gated, d_proj, far, weight, theirs = conv(
        ids, projected, tail, head, d_gated, taps, back, ahead, weight, cross
    )
    d_tokens, grad = sum_up(ids, d_proj, far, weight, mine, theirs)
    return gated, d_tokens, grad * (1.0 / math.sqrt(seq_total))


def solution(mesh):
    placed = (P("row", "col"), P(), P("row", "col"), P(None, "col"), P("row", "col"))
    return jax.shard_map(
        body,
        mesh=mesh,
        in_specs=placed,
        out_specs=(P("row", "col"), P("row", "col"), P("row", "col")),
        check_vma=False,
    )
```

```python
import functools
import math

import jax
import jax.numpy as jnp
from jax import lax
from jax.experimental import pallas as pl
from jax.experimental.pallas import tpu as pltpu
from jax.sharding import PartitionSpec as P

BF = jnp.bfloat16
F32 = jnp.float32
NY, NX, NC, NZ = 4, 4, 2, 8
TILE = 16
LANES = 128


def row_of(y, x, c):
    return ((y % NY) * NX + x % NX) * NC + c % NC


CHIPS = [(y, x) for y in range(NY) for x in range(NX)]
def around_z(value, steps):
    pairs = []
    for y, x in CHIPS:
        for c in range(NC):
            for z in range(NZ):
                to = (z + steps * (1 - 2 * c)) % NZ
                pairs.append((row_of(y, x, c) * NZ + z, row_of(y, x, c) * NZ + to))
    return lax.ppermute(value, ("row", "col"), pairs)


def narrow(value, steps):
    pairs = []
    for y, x in CHIPS:
        pairs.append((row_of(y, x, 0), row_of(y, x + steps, 0)))
        pairs.append((row_of(y, x, 1), row_of(y + steps, x, 1)))
    return lax.ppermute(value, "row", pairs)


def wide(value, steps):
    pairs = []
    for y, x in CHIPS:
        pairs.append((row_of(y, x, 0), row_of(y + steps, x, 0)))
        pairs.append((row_of(y, x, 1), row_of(y, x + steps, 1)))
    return lax.ppermute(value, "row", pairs)


def to_other_core(value):
    return lax.ppermute(value, "row", [(row_of(y, x, c), row_of(y, x, c + 1)) for y, x in CHIPS for c in range(NC)])


def next_row(value, steps):
    count = NY * NX * NC
    return lax.ppermute(value, "row", [(r, (r + steps) % count) for r in range(count)])


def live_taps(contig_lengths, first_row, rows):
    ends = jnp.cumsum(contig_lengths)
    starts = ends - contig_lengths
    at = first_row + jnp.arange(rows, dtype=jnp.int32)
    start = jnp.max(jnp.where(starts[None, :] <= at[:, None], starts[None, :], 0), axis=1)
    end = jnp.min(jnp.where(ends[None, :] > at[:, None], ends[None, :], 1 << 30), axis=1)
    back = jnp.minimum(at - start, 127)
    ahead = jnp.minimum(end - 1 - at, 127)
    wide = lambda v: jnp.broadcast_to(v.astype(BF)[:, None], (rows, LANES))
    return wide(back), wide(ahead)


def after(value, *others):
    return lax.optimization_barrier((value, others))[0]


VMEM = pl.BlockSpec(memory_space=pltpu.VMEM)
SMEM = pl.BlockSpec(memory_space=pltpu.SMEM)
HBM = pl.BlockSpec(memory_space=pltpu.HBM)


def loop(count, step):
    def run(i, carry):
        step(i)
        return carry

    lax.fori_loop(jnp.int32(0), jnp.int32(count), run, jnp.int32(0))


def add_kernel(a, b, out):
    out[...] = (a[...].astype(F32) + b[...].astype(F32)).astype(BF)


def add(a, b):
    return pl.pallas_call(
        add_kernel,
        in_specs=[VMEM] * 2,
        out_specs=VMEM,
        out_shape=jax.ShapeDtypeStruct(a.shape, BF),
        compiler_params=pltpu.CompilerParams(vmem_limit_bytes=2 << 20),
        cost_estimate=pl.CostEstimate(flops=1 << 20, bytes_accessed=1 << 20, transcendentals=0),
        name="add",
    )(a, b)


def stack_kernel(first, *refs):
    for k in range(4):
        refs[4][lax.rem(first[0] + k, 4)] = refs[k][...]


def stack(first, pieces):
    return pl.pallas_call(
        stack_kernel,
        in_specs=[SMEM] + [VMEM] * 4,
        out_specs=VMEM,
        out_shape=jax.ShapeDtypeStruct((4, 128, 512), BF),
        compiler_params=pltpu.CompilerParams(vmem_limit_bytes=2 << 20),
        cost_estimate=pl.CostEstimate(flops=1 << 20, bytes_accessed=1 << 20, transcendentals=0),
        name="stack",
    )(first, *pieces)


def sum_kernel(*refs):
    for j in range(4):
        total = refs[0][j].astype(F32)
        for k in range(1, 4):
            total += refs[k][j].astype(F32)
        refs[4 + j][...] = total.astype(BF)


def sum_four(blocks):
    return pl.pallas_call(
        sum_kernel,
        in_specs=[VMEM] * 4,
        out_specs=[VMEM] * 4,
        out_shape=[jax.ShapeDtypeStruct((128, 512), BF)] * 4,
        compiler_params=pltpu.CompilerParams(vmem_limit_bytes=4 << 20),
        cost_estimate=pl.CostEstimate(flops=1 << 20, bytes_accessed=1 << 20, transcendentals=0),
        name="sum_four",
    )(*blocks)


def place_of(ids, steps):
    return lax.rem(ids[3] + jnp.where(ids[2] == 0, steps, NZ - steps), NZ)


def load_weight(ids, own, other, w, sems, act):
    def one_core(core, blocks, base):
        for i, block in enumerate(blocks):
            if core == 0:
                y = lax.rem(ids[0] + i, 4)
                for half in range(2):
                    at = w.at[2 * y + half, :, 0]
                    act(pltpu.make_async_copy(block.at[2 * half : 2 * half + 2], at, sems.at[base + 2 * i + half]))
            else:
                x = lax.rem(ids[1] + i, 4)
                for y in range(4):
                    at = w.at[2 * y + x // 2, lax.rem(x, 2), 1]
                    act(pltpu.make_async_copy(block.at[y], at, sems.at[base + 4 * i + y]))

    @pl.when(ids[2] == 0)
    def _():
        one_core(0, own, 0)
        one_core(1, other, 8)

    @pl.when(ids[2] == 1)
    def _():
        one_core(0, other, 0)
        one_core(1, own, 8)


def start(copy):
    copy.start()


def wait(copy):
    copy.wait()


def start(copy):
    copy.start()


def wait(copy):
    copy.wait()


def split_piece(ids, k, piece, mine_ref, cross_ref):
    for core, out in ((ids[2], mine_ref), (1 - ids[2], cross_ref)):
        for xp in range(2):
            lanes = pl.ds(pl.multiple_of(xp * 256 + core * 128, 128), 128)
            out[k, :, xp * 128 : xp * 128 + 128] = piece[:, lanes]


def piece_term(ids, k, piece, w):
    return jnp.dot(piece[...], w[place_of(ids, k)].reshape(512, 512), preferred_element_type=F32)


FIRST, NEXT, LATE = (0, 1, 7, 2, 6), (3, 5), 4


def split_kernel(ids, *refs):
    pieces, (tok, mine_ref, cross_ref) = refs[0:5], refs[5:]
    for n, k in enumerate(FIRST):
        tok[n] = pieces[n][...]
        split_piece(ids, k, pieces[n], mine_ref, cross_ref)


def split_tokens(ids, pieces):
    return pl.pallas_call(
        split_kernel,
        in_specs=[SMEM] + [VMEM] * 5,
        out_specs=[VMEM] * 3,
        out_shape=[jax.ShapeDtypeStruct((n, 256, lanes), BF) for n, lanes in ((5, 512), (NZ, 256), (NZ + 2, 256))],
        compiler_params=pltpu.CompilerParams(vmem_limit_bytes=4 << 20),
        cost_estimate=pl.CostEstimate(flops=1 << 20, bytes_accessed=4 << 20, transcendentals=0),
        name="split_tokens",
    )(ids, *pieces)


def early_kernel(ids, tok, q3, p3, *refs):
    own, other, (_, _, acc, w, mine_ref, cross_ref, more, sems, tok_sems) = refs[0:4], refs[4:8], refs[8:]
    load_weight(ids, own, other, w, sems, start)
    arrive = [pltpu.make_async_copy(piece, more.at[n], tok_sems.at[n]) for n, piece in enumerate((q3, p3))]
    for copy in arrive:
        copy.start()
    for copy in arrive:
        copy.wait()
    for n, k in enumerate(NEXT):
        split_piece(ids, k, more.at[n], mine_ref, cross_ref)
    load_weight(ids, own, other, w, sems, wait)
    total = None
    for k, piece in zip(FIRST + NEXT, [tok.at[n] for n in range(5)] + [more.at[0], more.at[1]]):
        term = piece_term(ids, k, piece, w)
        total = term if total is None else total + term
    acc[...] = total


def late_kernel(ids, *refs):
    piece, acc, w, _, _, dg_ref, p_ref, tail_ref, head_ref, mine_ref, cross_ref = refs
    total = acc[...] + piece_term(ids, LATE, piece, w)
    split_piece(ids, LATE, piece, mine_ref, cross_ref)
    p = total.astype(BF)
    p_ref[...] = p
    tail_ref[...] = p[128:256]
    top = p[0:128].astype(F32)
    head_ref[...] = (dg_ref[0:128].astype(F32) * (top * jax.nn.sigmoid(top))).astype(BF)


def project_early(ids, tok, pieces, blocks, mine, cross):
    return pl.pallas_call(
        early_kernel,
        in_specs=[SMEM, VMEM] + [HBM] * 10 + [VMEM] * 2,
        out_specs=[VMEM] * 4,
        out_shape=[
            jax.ShapeDtypeStruct((256, 512), F32),
            jax.ShapeDtypeStruct((NZ, 2, 2, 128, 512), BF),
            jax.ShapeDtypeStruct(mine.shape, BF),
            jax.ShapeDtypeStruct(cross.shape, BF),
        ],
        input_output_aliases={12: 2, 13: 3},
        scratch_shapes=[
            pltpu.VMEM((2, 256, 512), BF),
            pltpu.SemaphoreType.DMA((24,)),
            pltpu.SemaphoreType.DMA((2,)),
        ],
        compiler_params=pltpu.CompilerParams(vmem_limit_bytes=6 << 20),
        cost_estimate=pl.CostEstimate(flops=1 << 32, bytes_accessed=8 << 20, transcendentals=0),
        name="project_early",
    )(ids, tok, *pieces, *blocks, mine, cross)


def project_late(ids, piece, early, d_gated):
    half = jax.ShapeDtypeStruct((128, 512), BF)
    part_of, more = jax.ShapeDtypeStruct((NZ, 256, 256), BF), jax.ShapeDtypeStruct((NZ + 2, 256, 256), BF)
    return pl.pallas_call(
        late_kernel,
        in_specs=[SMEM] + [VMEM] * 6,
        out_specs=[VMEM] * 5,
        out_shape=[jax.ShapeDtypeStruct((256, 512), BF), half, half, part_of, more],
        input_output_aliases={4: 3, 5: 4},
        compiler_params=pltpu.CompilerParams(vmem_limit_bytes=6 << 20),
        cost_estimate=pl.CostEstimate(flops=2 * 256 * 512 * 512, bytes_accessed=4 << 20, transcendentals=0),
        name="project_late",
    )(ids, piece, *early, d_gated)


def mix(ext, live_ref, taps_ref, even, odd, acc, reverse):
    acc[...] = jnp.zeros_like(acc)
    rows = ext.shape[0]
    zero, one = jnp.zeros((), BF), jnp.ones((), BF)

    def shift(b):
        r = ext[...]
        even[...] = r.astype(BF)
        odd[...] = jnp.concatenate([r[8:], r[:8]] if reverse else [r[-8:], r[:-8]], 0).astype(BF)
        ext[...] = pltpu.roll(r, rows - 1 if reverse else 1, 0)
        for u in range(8):
            at = slice(TILE * u, TILE * u + TILE)
            live = live_ref[at] - b.astype(F32).astype(BF)
            total = None
            for k in range(16):
                v = u + k // 2 if reverse else u + 8 - k // 2
                source = (odd if k % 2 else even)[TILE * v : TILE * v + TILE]
                m = jnp.minimum(jnp.maximum(live - jnp.array(8 * k - 1, BF), zero), one)
                term = source * taps_ref[b, k] * jnp.concatenate([m] * 4, 1)
                total = term if total is None else total + term
            acc[at] += total.astype(F32)

    loop(8, shift)


def gates(p, up, out):
    sigma = jax.nn.sigmoid(p)
    gate = p * sigma
    return (out * gate).astype(BF), up * out * (sigma * (1.0 + p * (1.0 - sigma))), up * gate


LOW, HIGH = slice(0, 128), slice(128, 256)


def ahead_inside_kernel(p_ref, dg_ref, taps_ref, live_ref, gated_ref, dgate_ref, ext, even, odd, acc):
    ext[...] = p_ref[...].astype(F32)
    mix(ext, live_ref.at[HIGH], taps_ref, even, odd, acc, False)
    p, up = p_ref[HIGH].astype(F32), dg_ref[HIGH].astype(F32)
    gated_ref[...], dgate_ref[...], _ = gates(p, up, acc[...])


def back_inside_kernel(p_ref, dg_ref, taps_ref, live_ref, part_ref, dconv_ref, ext, even, odd, acc):
    p = p_ref[...].astype(F32)
    ext[...] = dg_ref[...].astype(F32) * (p * jax.nn.sigmoid(p))
    dconv_ref[...] = ext[HIGH]
    mix(ext, live_ref.at[LOW], taps_ref, even, odd, acc, True)
    part_ref[...] = acc[...]


def ahead_edge_kernel(p_ref, dg_ref, taps_ref, live_ref, tail_ref, gated_hi, part_ref, gated_ref, low_ref, ext, even, odd, acc):
    p, up = p_ref[LOW].astype(F32), dg_ref[LOW].astype(F32)
    ext[LOW] = tail_ref[...].astype(F32)
    ext[HIGH] = p
    mix(ext, live_ref.at[LOW], taps_ref, even, odd, acc, False)
    gated_ref[LOW], d_gate, _ = gates(p, up, acc[...])
    gated_ref[HIGH] = gated_hi[...]
    low_ref[...] = (part_ref[...] + d_gate).astype(BF)


def back_edge_kernel(
    dconv_ref, head_ref, taps_ref, live_ref, low_ref, dgate_ref, ids, w_ref, _, dproj_ref, far_ref, w, cross_ref,
    ext, even, odd, acc, sem,
):
    load = pltpu.make_async_copy(w_ref, w, sem)
    load.start()
    ext[LOW] = dconv_ref[...]
    ext[HIGH] = head_ref[...].astype(F32)
    mix(ext, live_ref.at[HIGH], taps_ref, even, odd, acc, True)
    dproj_ref[LOW] = low_ref[...]
    dproj_ref[HIGH] = (acc[...] + dgate_ref[...]).astype(BF)
    cross_ref[NZ] = dproj_ref[:, 0:256]
    cross_ref[NZ + 1] = dproj_ref[:, 256:512]
    load.wait()
    far_ref[...] = back_term(dproj_ref[...], w[place_of(ids, 4)].reshape(512, 512))


def back_term(d, block):
    return lax.dot_general(d, block, (((1,), (1,)), ((), ())), preferred_element_type=F32).astype(BF)


def mix_call(kernel, name, shapes, *operands, specs=None, scratch=(), aliases={}):
    return pl.pallas_call(
        kernel,
        in_specs=specs or [VMEM] * len(operands),
        out_specs=[VMEM] * len(shapes),
        out_shape=[jax.ShapeDtypeStruct(shape, kind) for shape, kind in shapes],
        scratch_shapes=[
            pltpu.VMEM((256, 512), F32),
            pltpu.VMEM((256, 512), BF),
            pltpu.VMEM((256, 512), BF),
            pltpu.VMEM((128, 512), F32),
            *scratch,
        ],
        input_output_aliases=aliases,
        compiler_params=pltpu.CompilerParams(vmem_limit_bytes=8 << 20),
        cost_estimate=pl.CostEstimate(flops=1 << 32, bytes_accessed=4 << 20, transcendentals=0),
        name=name,
    )(*operands)


def conv(ids, p, tail, head, d_gated, taps, back, ahead, w, cross):
    half, whole = (128, 512), (256, 512)
    tail = next_row(tail, 1)
    gated_hi, dgate_hi = mix_call(
        ahead_inside_kernel, "ahead_inside", [(half, BF), (half, F32)], p, d_gated, taps, back
    )
    head = next_row(after(head, gated_hi), -1)
    part, dconv_hi = mix_call(
        back_inside_kernel, "back_inside", [(half, F32), (half, F32)], p, d_gated, taps, ahead
    )
    gated, low = mix_call(
        ahead_edge_kernel, "ahead_edge", [(whole, BF), (half, BF)], p, d_gated, taps, back, tail, gated_hi, part
    )
    d_proj, far, w, cross = mix_call(
        back_edge_kernel, "back_edge", [(whole, BF), (whole, BF), (w.shape, BF), (cross.shape, BF)],
        dconv_hi, head, taps, ahead, low, dgate_hi, ids, w, cross,
        specs=[VMEM] * 6 + [SMEM, HBM, VMEM], scratch=[pltpu.SemaphoreType.DMA], aliases={8: 3},
    )
    return gated, d_proj, far, w, cross


NEAR = (3, 5, 2, 6, 1, 7, 0)


def near_kernel(ids, d_ref, w, *outs):
    d = d_ref[...]
    for steps, out in zip(NEAR, outs):
        out[...] = back_term(d, w[place_of(ids, steps)].reshape(512, 512))


def near_terms(ids, d_proj, weight):
    return pl.pallas_call(
        near_kernel,
        in_specs=[SMEM, VMEM, VMEM],
        out_specs=[VMEM] * 7,
        out_shape=[jax.ShapeDtypeStruct((256, 512), BF)] * 7,
        compiler_params=pltpu.CompilerParams(vmem_limit_bytes=4 << 20),
        cost_estimate=pl.CostEstimate(flops=2 * 256 * 512 * 512 * 7, bytes_accessed=6 << 20, transcendentals=0),
        name="near_terms",
    )(ids, d_proj, weight)


def add_three_kernel(a, b, c, out):
    out[...] = (a[...].astype(F32) + b[...].astype(F32) + c[...].astype(F32)).astype(BF)


def add_three(a, b, c):
    return pl.pallas_call(
        add_three_kernel,
        in_specs=[VMEM] * 3,
        out_specs=VMEM,
        out_shape=jax.ShapeDtypeStruct(a.shape, BF),
        compiler_params=pltpu.CompilerParams(vmem_limit_bytes=2 << 20),
        cost_estimate=pl.CostEstimate(flops=1 << 34, bytes_accessed=1 << 20, transcendentals=0),
        name="add_three",
    )(a, b, c)


def grad_kernel(ids, mine, theirs, d_mine, *refs):
    outs, out, d_theirs = refs[:4], refs[4], refs[5]
    d_theirs[:, 0:256] = theirs[NZ]
    d_theirs[:, 256:512] = theirs[NZ + 1]
    me = ids[2]
    dims = (((0,), (0,)), ((), ()))
    for k in range(NZ):
        zb = place_of(ids, k)
        total = lax.dot_general(mine[k], d_mine[...], dims, preferred_element_type=F32)
        total += lax.dot_general(theirs[(NZ - k) % NZ], d_theirs[...], dims, preferred_element_type=F32)
        total = total.astype(BF)
        for xp in range(2):
            dy = lax.rem(zb // 2 + 4 - ids[0], 4)
            dx = lax.rem(lax.rem(zb, 2) * 2 + xp + 4 - ids[1], 4)
            out[jnp.where(me == 0, dy, dx), jnp.where(me == 0, dx, dy)] = total[xp * 128 : xp * 128 + 128]
    for k in range(4):
        outs[k][...] = out[k]


def weight_terms(ids, mine, theirs, d_mine):
    return pl.pallas_call(
        grad_kernel,
        in_specs=[SMEM] + [VMEM] * 3,
        out_specs=[VMEM] * 4,
        out_shape=[jax.ShapeDtypeStruct((4, 128, 512), BF)] * 4,
        scratch_shapes=[pltpu.VMEM((4, 4, 128, 512), BF), pltpu.VMEM((256, 512), BF)],
        compiler_params=pltpu.CompilerParams(vmem_limit_bytes=6 << 20),
        cost_estimate=pl.CostEstimate(flops=2 * 512 * 2048 * 512, bytes_accessed=5 << 20, transcendentals=0),
        name="weight_terms",
    )(ids, mine, theirs, d_mine)


def sum_up(ids, d_proj, far, weight, mine, cross):
    p = around_z(far, 1)
    theirs = to_other_core(cross)
    p3, q3, p2, q2, p1, q1, own = near_terms(ids, d_proj, weight)
    q = around_z(q3, -1)
    g = weight_terms(ids, mine, after(theirs, own), d_proj)
    p = around_z(add(after(p3, g[0]), p), 1)
    s = [g[0]] + [wide(g[k], k) for k in (1, 2, 3)]
    q = around_z(add(q2, q), -1)
    p = around_z(add(p2, p), 1)
    q_last = add(q1, q)
    q = around_z(q_last, -1)
    p_last = add(p1, p)
    p = around_z(p_last, 1)
    n = sum_four([after(s[0], p_last, q_last)] + s[1:])
    n = [n[0]] + [narrow(n[k], k) for k in (1, 2, 3)]
    d_tokens = add_three(own, p, q)
    return d_tokens, sum(v.astype(F32) for v in after(n, d_tokens))


def body(tokens, contig_lengths, w_in, conv_filter, d_gated):
    rows = tokens.shape[0]
    seq_total = rows * NY * NX * NC
    row, z = lax.axis_index("row"), lax.axis_index("col")
    core, chip = row % NC, row // NC
    y, x = chip // NX, chip % NX
    ids = jnp.stack([y, x, core, z]).astype(jnp.int32)

    w = [narrow(w_in, 4 - k) for k in (1, 2, 3)]
    p1, q1 = around_z(tokens, 1), around_z(tokens, -1)
    first = jnp.where(core == 0, x, y).astype(jnp.int32).reshape(1)
    row_block = stack(first, [w_in] + w)
    own = [row_block] + [wide(row_block, 4 - k) for k in (1, 2, 3)]
    p2, q2 = around_z(p1, 1), around_z(q1, -1)
    conv_filter, contig_lengths = after((conv_filter, contig_lengths), q1)
    back, ahead = live_taps(contig_lengths, row * rows, rows)
    taps = conv_filter.astype(BF).reshape(16, 8, 1, 512).transpose(1, 0, 2, 3)
    taps = jnp.broadcast_to(taps, (8, 16, TILE, 512))
    p3, q3 = around_z(p2, 1), around_z(q2, -1)
    tok, mine, cross = split_tokens(ids, [tokens, q1, p1, q2, p2])
    other = [to_other_core(block) for block in after(own, p3, q3, back, ahead, taps, tok)]
    p4 = around_z(p3, 1)
    early = project_early(ids, tok, [q3, p3], own + other, mine, cross)
    weight = early[1]
    projected, tail, head, mine, cross = project_late(ids, p4, early, d_gated)
    gated, d_proj, far, weight, cross = conv(
        ids, projected, tail, head, d_gated, taps, back, ahead, weight, cross
    )
    d_tokens, grad = sum_up(ids, d_proj, far, weight, mine, cross)
    return gated, d_tokens, grad * (1.0 / math.sqrt(seq_total))


def solution(mesh):
    placed = (P("row", "col"), P(), P("row", "col"), P(None, "col"), P("row", "col"))
    return jax.shard_map(
        body,
        mesh=mesh,
        in_specs=placed,
        out_specs=(P("row", "col"), P("row", "col"), P("row", "col")),
        check_vma=False,
    )
```

```python
import functools
import math

import jax
import jax.numpy as jnp
from jax import lax
from jax.experimental import pallas as pl
from jax.experimental.pallas import tpu as pltpu
from jax.sharding import PartitionSpec as P

BF = jnp.bfloat16
F32 = jnp.float32
NY, NX, NC, NZ = 4, 4, 2, 8
TILE = 16
LANES = 128


def row_of(y, x, c):
    return ((y % NY) * NX + x % NX) * NC + c % NC


CHIPS = [(y, x) for y in range(NY) for x in range(NX)]
def around_z(value, steps):
    pairs = []
    for y, x in CHIPS:
        for c in range(NC):
            for z in range(NZ):
                to = (z + steps * (1 - 2 * c)) % NZ
                pairs.append((row_of(y, x, c) * NZ + z, row_of(y, x, c) * NZ + to))
    return lax.ppermute(value, ("row", "col"), pairs)


def narrow(value, steps):
    pairs = []
    for y, x in CHIPS:
        pairs.append((row_of(y, x, 0), row_of(y, x + steps, 0)))
        pairs.append((row_of(y, x, 1), row_of(y + steps, x, 1)))
    return lax.ppermute(value, "row", pairs)


def wide(value, steps):
    pairs = []
    for y, x in CHIPS:
        pairs.append((row_of(y, x, 0), row_of(y + steps, x, 0)))
        pairs.append((row_of(y, x, 1), row_of(y, x + steps, 1)))
    return lax.ppermute(value, "row", pairs)


def to_other_core(value):
    return lax.ppermute(value, "row", [(row_of(y, x, c), row_of(y, x, c + 1)) for y, x in CHIPS for c in range(NC)])


def next_row(value, steps):
    count = NY * NX * NC
    return lax.ppermute(value, "row", [(r, (r + steps) % count) for r in range(count)])


def live_taps(contig_lengths, first_row, rows):
    ends = jnp.cumsum(contig_lengths)
    starts = ends - contig_lengths
    at = first_row + jnp.arange(rows, dtype=jnp.int32)
    start = jnp.max(jnp.where(starts[None, :] <= at[:, None], starts[None, :], 0), axis=1)
    end = jnp.min(jnp.where(ends[None, :] > at[:, None], ends[None, :], 1 << 30), axis=1)
    back = jnp.minimum(at - start, 127)
    ahead = jnp.minimum(end - 1 - at, 127)
    wide = lambda v: jnp.broadcast_to(v.astype(BF)[:, None], (rows, LANES))
    return wide(back), wide(ahead)


def after(value, *others):
    return lax.optimization_barrier((value, others))[0]


VMEM = pl.BlockSpec(memory_space=pltpu.VMEM)
SMEM = pl.BlockSpec(memory_space=pltpu.SMEM)
HBM = pl.BlockSpec(memory_space=pltpu.HBM)


def loop(count, step):
    def run(i, carry):
        step(i)
        return carry

    lax.fori_loop(jnp.int32(0), jnp.int32(count), run, jnp.int32(0))


def add_kernel(a, b, out):
    out[...] = (a[...].astype(F32) + b[...].astype(F32)).astype(BF)


def add(a, b):
    return pl.pallas_call(
        add_kernel,
        in_specs=[VMEM] * 2,
        out_specs=VMEM,
        out_shape=jax.ShapeDtypeStruct(a.shape, BF),
        compiler_params=pltpu.CompilerParams(vmem_limit_bytes=2 << 20),
        cost_estimate=pl.CostEstimate(flops=1 << 20, bytes_accessed=1 << 20, transcendentals=0),
        name="add",
    )(a, b)


def stack_kernel(first, *refs):
    for k in range(4):
        refs[4][lax.rem(first[0] + k, 4)] = refs[k][...]


def stack(first, pieces):
    return pl.pallas_call(
        stack_kernel,
        in_specs=[SMEM] + [VMEM] * 4,
        out_specs=VMEM,
        out_shape=jax.ShapeDtypeStruct((4, 128, 512), BF),
        compiler_params=pltpu.CompilerParams(vmem_limit_bytes=2 << 20),
        cost_estimate=pl.CostEstimate(flops=1 << 20, bytes_accessed=1 << 20, transcendentals=0),
        name="stack",
    )(first, *pieces)


def sum_kernel(*refs):
    for j in range(4):
        total = refs[0][j].astype(F32)
        for k in range(1, 4):
            total += refs[k][j].astype(F32)
        refs[4 + j][...] = total.astype(BF)


def sum_four(blocks):
    return pl.pallas_call(
        sum_kernel,
        in_specs=[VMEM] * 4,
        out_specs=[VMEM] * 4,
        out_shape=[jax.ShapeDtypeStruct((128, 512), BF)] * 4,
        compiler_params=pltpu.CompilerParams(vmem_limit_bytes=4 << 20),
        cost_estimate=pl.CostEstimate(flops=1 << 20, bytes_accessed=1 << 20, transcendentals=0),
        name="sum_four",
    )(*blocks)


def place_of(ids, steps):
    return lax.rem(ids[3] + jnp.where(ids[2] == 0, steps, NZ - steps), NZ)


def load_weight(ids, core, blocks, w, sems, act):
    @pl.when(core == 0)
    def _():
        for i, block in enumerate(blocks):
            act(pltpu.make_async_copy(block, w.at[lax.rem(ids[0] + i, 4), :, 0], sems.at[i]))

    @pl.when(core == 1)
    def _():
        for i, block in enumerate(blocks):
            act(pltpu.make_async_copy(block, w.at[:, lax.rem(ids[1] + i, 4), 1], sems.at[i]))


def weight_rows(ids, k, w):
    zb = place_of(ids, k)
    return w.at[zb // 2, pl.ds(lax.rem(zb, 2) * 2, 2)]


def start(copy):
    copy.start()


def wait(copy):
    copy.wait()


def start(copy):
    copy.start()


def wait(copy):
    copy.wait()


def split_piece(ids, k, piece, mine_ref, cross_ref):
    for core, out in ((ids[2], mine_ref), (1 - ids[2], cross_ref)):
        for xp in range(2):
            lanes = pl.ds(pl.multiple_of(xp * 256 + core * 128, 128), 128)
            out[k, :, xp * 128 : xp * 128 + 128] = piece[:, lanes]


FIRST, NEXT = (0, 1, 7, 2, 6), (3, 5, 4)


def split_kernel(ids, *refs):
    pieces, (mine_ref, cross_ref) = refs[0:5], refs[5:]
    for n, k in enumerate(FIRST):
        split_piece(ids, k, pieces[n], mine_ref, cross_ref)


def split_tokens(ids, pieces):
    return pl.pallas_call(
        split_kernel,
        in_specs=[SMEM] + [VMEM] * 5,
        out_specs=[VMEM] * 2,
        out_shape=[jax.ShapeDtypeStruct((n, 256, 256), BF) for n in (NZ, NZ + 2)],
        compiler_params=pltpu.CompilerParams(vmem_limit_bytes=4 << 20),
        cost_estimate=pl.CostEstimate(flops=1 << 20, bytes_accessed=4 << 20, transcendentals=0),
        name="split_tokens",
    )(ids, *pieces)


def core_term(ids, core, columns, w):
    total = None
    for k in range(NZ):
        rows = weight_rows(ids, k, w)[:, core].reshape(256, 512)
        term = jnp.dot(columns[k], rows, preferred_element_type=F32)
        total = term if total is None else total + term
    return total


def own_kernel(ids, *refs):
    pieces, own, (_, _, acc, w, mine_ref, cross_ref, sems) = refs[0:3], refs[3:7], refs[7:]
    load_weight(ids, ids[2], own, w, sems, start)
    for piece, k in zip(pieces, NEXT):
        split_piece(ids, k, piece, mine_ref, cross_ref)
    load_weight(ids, ids[2], own, w, sems, wait)
    acc[...] = core_term(ids, ids[2], mine_ref, w)


def project_own(ids, pieces, own, mine, cross):
    return pl.pallas_call(
        own_kernel,
        in_specs=[SMEM] + [VMEM] * 3 + [HBM] * 4 + [VMEM] * 2,
        out_specs=[VMEM] * 4,
        out_shape=[
            jax.ShapeDtypeStruct((256, 512), F32),
            jax.ShapeDtypeStruct((4, 4, 2, 128, 512), BF),
            jax.ShapeDtypeStruct(mine.shape, BF),
            jax.ShapeDtypeStruct(cross.shape, BF),
        ],
        input_output_aliases={8: 2, 9: 3},
        scratch_shapes=[pltpu.SemaphoreType.DMA((4,))],
        compiler_params=pltpu.CompilerParams(vmem_limit_bytes=6 << 20),
        cost_estimate=pl.CostEstimate(flops=1 << 32, bytes_accessed=4 << 20, transcendentals=0),
        name="project_own",
    )(ids, *pieces, *own, mine, cross)


def other_kernel(ids, *refs):
    other, (cross, acc, _, dg_ref, p_ref, tail_ref, head_ref, w, sems) = refs[0:4], refs[4:]
    load_weight(ids, 1 - ids[2], other, w, sems, start)
    load_weight(ids, 1 - ids[2], other, w, sems, wait)
    p = (acc[...] + core_term(ids, 1 - ids[2], cross, w)).astype(BF)
    p_ref[...] = p
    tail_ref[...] = p[128:256]
    top = p[0:128].astype(F32)
    head_ref[...] = (dg_ref[0:128].astype(F32) * (top * jax.nn.sigmoid(top))).astype(BF)


def project_other(ids, other, cross, acc, w, d_gated):
    half = jax.ShapeDtypeStruct((128, 512), BF)
    return pl.pallas_call(
        other_kernel,
        in_specs=[SMEM] + [HBM] * 4 + [VMEM] * 4,
        out_specs=[VMEM] * 4,
        out_shape=[jax.ShapeDtypeStruct((256, 512), BF), half, half, jax.ShapeDtypeStruct(w.shape, BF)],
        input_output_aliases={7: 3},
        scratch_shapes=[pltpu.SemaphoreType.DMA((4,))],
        compiler_params=pltpu.CompilerParams(vmem_limit_bytes=6 << 20),
        cost_estimate=pl.CostEstimate(flops=1 << 30, bytes_accessed=4 << 20, transcendentals=0),
        name="project_other",
    )(ids, *other, cross, acc, w, d_gated)


def mix(ext, live_ref, taps_ref, even, odd, acc, reverse):
    acc[...] = jnp.zeros_like(acc)
    rows = ext.shape[0]
    zero, one = jnp.zeros((), BF), jnp.ones((), BF)

    def shift(b):
        r = ext[...]
        even[...] = r.astype(BF)
        odd[...] = jnp.concatenate([r[8:], r[:8]] if reverse else [r[-8:], r[:-8]], 0).astype(BF)
        ext[...] = pltpu.roll(r, rows - 1 if reverse else 1, 0)
        for u in range(8):
            at = slice(TILE * u, TILE * u + TILE)
            live = live_ref[at] - b.astype(F32).astype(BF)
            total = None
            for k in range(16):
                v = u + k // 2 if reverse else u + 8 - k // 2
                source = (odd if k % 2 else even)[TILE * v : TILE * v + TILE]
                m = jnp.minimum(jnp.maximum(live - jnp.array(8 * k - 1, BF), zero), one)
                term = source * taps_ref[b, k] * jnp.concatenate([m] * 4, 1)
                total = term if total is None else total + term
            acc[at] += total.astype(F32)

    loop(8, shift)


def gates(p, up, out):
    sigma = jax.nn.sigmoid(p)
    gate = p * sigma
    return (out * gate).astype(BF), up * out * (sigma * (1.0 + p * (1.0 - sigma))), up * gate


LOW, HIGH = slice(0, 128), slice(128, 256)


def inside_kernel(
    p_ref, dg_ref, taps_ref, back_ref, ahead_ref, gated_ref, dgate_ref, part_ref, dconv_ref, ext, even, odd, acc
):
    ext[...] = p_ref[...].astype(F32)
    mix(ext, back_ref.at[HIGH], taps_ref, even, odd, acc, False)
    p, up = p_ref[HIGH].astype(F32), dg_ref[HIGH].astype(F32)
    gated_ref[...], dgate_ref[...], ext[HIGH] = gates(p, up, acc[...])
    p, up = p_ref[LOW].astype(F32), dg_ref[LOW].astype(F32)
    ext[LOW] = up * (p * jax.nn.sigmoid(p))
    dconv_ref[...] = ext[HIGH]
    mix(ext, ahead_ref.at[LOW], taps_ref, even, odd, part_ref, True)


def edges_kernel(
    p_ref, dg_ref, taps_ref, back_ref, ahead_ref, tail_ref, head_ref, gated_hi, dgate_ref, part_ref, dconv_ref,
    ids, w_ref, _, gated_ref, dproj_ref, far_ref, w, cross_ref, ext, even, odd, acc, sem,
):
    load = pltpu.make_async_copy(w_ref, w, sem)
    load.start()
    p, up = p_ref[LOW].astype(F32), dg_ref[LOW].astype(F32)
    ext[LOW] = tail_ref[...].astype(F32)
    ext[HIGH] = p
    mix(ext, back_ref.at[LOW], taps_ref, even, odd, acc, False)
    gated_ref[LOW], d_gate, _ = gates(p, up, acc[...])
    gated_ref[HIGH] = gated_hi[...]
    dproj_ref[LOW] = (part_ref[...] + d_gate).astype(BF)
    ext[LOW] = dconv_ref[...]
    ext[HIGH] = head_ref[...].astype(F32)
    mix(ext, ahead_ref.at[HIGH], taps_ref, even, odd, acc, True)
    dproj_ref[HIGH] = (acc[...] + dgate_ref[...]).astype(BF)
    cross_ref[NZ] = dproj_ref[:, 0:256]
    cross_ref[NZ + 1] = dproj_ref[:, 256:512]
    load.wait()
    far_ref[...] = back_term(dproj_ref[...], weight_rows(ids, 4, w)[...].reshape(512, 512))


def back_term(d, block):
    return lax.dot_general(d, block, (((1,), (1,)), ((), ())), preferred_element_type=F32).astype(BF)


def mix_call(kernel, name, shapes, *operands, specs=None, scratch=(), aliases={}):
    return pl.pallas_call(
        kernel,
        in_specs=specs or [VMEM] * len(operands),
        out_specs=[VMEM] * len(shapes),
        out_shape=[jax.ShapeDtypeStruct(shape, kind) for shape, kind in shapes],
        scratch_shapes=[
            pltpu.VMEM((256, 512), F32),
            pltpu.VMEM((256, 512), BF),
            pltpu.VMEM((256, 512), BF),
            pltpu.VMEM((128, 512), F32),
            *scratch,
        ],
        input_output_aliases=aliases,
        compiler_params=pltpu.CompilerParams(vmem_limit_bytes=8 << 20),
        cost_estimate=pl.CostEstimate(flops=1 << 32, bytes_accessed=4 << 20, transcendentals=0),
        name=name,
    )(*operands)


def conv(ids, p, tail, head, d_gated, taps, back, ahead, w, cross):
    half, whole = (128, 512), (256, 512)
    tail, head = next_row(tail, 1), next_row(head, -1)
    inside = mix_call(
        inside_kernel, "inside", [(half, BF), (half, F32), (half, F32), (half, F32)], p, d_gated, taps, back, ahead
    )
    return mix_call(
        edges_kernel, "edges", [(whole, BF), (whole, BF), (whole, BF), (w.shape, BF), (cross.shape, BF)],
        p, d_gated, taps, back, ahead, tail, head, *inside, ids, w, cross,
        specs=[VMEM] * 11 + [SMEM, HBM, VMEM], scratch=[pltpu.SemaphoreType.DMA], aliases={13: 4},
    )


NEAR = (3, 5, 2, 6, 1, 7, 0)


def near_kernel(ids, d_ref, w, *outs):
    d = d_ref[...]
    for steps, out in zip(NEAR, outs):
        out[...] = back_term(d, weight_rows(ids, steps, w)[...].reshape(512, 512))


def near_terms(ids, d_proj, weight):
    return pl.pallas_call(
        near_kernel,
        in_specs=[SMEM, VMEM, VMEM],
        out_specs=[VMEM] * 7,
        out_shape=[jax.ShapeDtypeStruct((256, 512), BF)] * 7,
        compiler_params=pltpu.CompilerParams(vmem_limit_bytes=4 << 20),
        cost_estimate=pl.CostEstimate(flops=2 * 256 * 512 * 512 * 7, bytes_accessed=6 << 20, transcendentals=0),
        name="near_terms",
    )(ids, d_proj, weight)


def add_three_kernel(a, b, c, out):
    out[...] = (a[...].astype(F32) + b[...].astype(F32) + c[...].astype(F32)).astype(BF)


def add_three(a, b, c):
    return pl.pallas_call(
        add_three_kernel,
        in_specs=[VMEM] * 3,
        out_specs=VMEM,
        out_shape=jax.ShapeDtypeStruct(a.shape, BF),
        compiler_params=pltpu.CompilerParams(vmem_limit_bytes=2 << 20),
        cost_estimate=pl.CostEstimate(flops=1 << 34, bytes_accessed=1 << 20, transcendentals=0),
        name="add_three",
    )(a, b, c)


def grad_kernel(ids, mine, theirs, d_mine, *refs):
    outs, out, d_theirs = refs[:4], refs[4], refs[5]
    d_theirs[:, 0:256] = theirs[NZ]
    d_theirs[:, 256:512] = theirs[NZ + 1]
    me = ids[2]
    dims = (((0,), (0,)), ((), ()))
    for k in range(NZ):
        zb = place_of(ids, k)
        total = lax.dot_general(mine[k], d_mine[...], dims, preferred_element_type=F32)
        total += lax.dot_general(theirs[(NZ - k) % NZ], d_theirs[...], dims, preferred_element_type=F32)
        total = total.astype(BF)
        for xp in range(2):
            dy = lax.rem(zb // 2 + 4 - ids[0], 4)
            dx = lax.rem(lax.rem(zb, 2) * 2 + xp + 4 - ids[1], 4)
            out[jnp.where(me == 0, dy, dx), jnp.where(me == 0, dx, dy)] = total[xp * 128 : xp * 128 + 128]
    for k in range(4):
        outs[k][...] = out[k]


def weight_terms(ids, mine, theirs, d_mine):
    return pl.pallas_call(
        grad_kernel,
        in_specs=[SMEM] + [VMEM] * 3,
        out_specs=[VMEM] * 4,
        out_shape=[jax.ShapeDtypeStruct((4, 128, 512), BF)] * 4,
        scratch_shapes=[pltpu.VMEM((4, 4, 128, 512), BF), pltpu.VMEM((256, 512), BF)],
        compiler_params=pltpu.CompilerParams(vmem_limit_bytes=6 << 20),
        cost_estimate=pl.CostEstimate(flops=2 * 512 * 2048 * 512, bytes_accessed=5 << 20, transcendentals=0),
        name="weight_terms",
    )(ids, mine, theirs, d_mine)


def sum_up(ids, d_proj, far, weight, mine, cross):
    p = around_z(far, 1)
    theirs = to_other_core(cross)
    p3, q3, p2, q2, p1, q1, own = near_terms(ids, d_proj, weight)
    q = around_z(q3, -1)
    g = weight_terms(ids, mine, after(theirs, own), d_proj)
    p = around_z(add(after(p3, g[0]), p), 1)
    s = [g[0]] + [wide(g[k], k) for k in (1, 2, 3)]
    q = around_z(add(q2, q), -1)
    p = around_z(add(p2, p), 1)
    q_last = add(q1, q)
    q = around_z(q_last, -1)
    p_last = add(p1, p)
    p = around_z(p_last, 1)
    n = sum_four([after(s[0], p_last, q_last)] + s[1:])
    n = [n[0]] + [narrow(n[k], k) for k in (1, 2, 3)]
    d_tokens = add_three(own, p, q)
    return d_tokens, sum(v.astype(F32) for v in after(n, d_tokens))


def body(tokens, contig_lengths, w_in, conv_filter, d_gated):
    rows = tokens.shape[0]
    seq_total = rows * NY * NX * NC
    row, z = lax.axis_index("row"), lax.axis_index("col")
    core, chip = row % NC, row // NC
    y, x = chip // NX, chip % NX
    ids = jnp.stack([y, x, core, z]).astype(jnp.int32)

    w = [narrow(w_in, 4 - k) for k in (1, 2, 3)]
    p1, q1 = around_z(tokens, 1), around_z(tokens, -1)
    first = jnp.where(core == 0, x, y).astype(jnp.int32).reshape(1)
    row_block = stack(first, [w_in] + w)
    own = [row_block] + [wide(row_block, 4 - k) for k in (1, 2, 3)]
    p2, q2 = around_z(after(p1, row_block), 1), around_z(after(q1, row_block), -1)
    conv_filter, contig_lengths = after((conv_filter, contig_lengths), q1)
    back, ahead = live_taps(contig_lengths, row * rows, rows)
    taps = conv_filter.astype(BF).reshape(16, 8, 1, 512).transpose(1, 0, 2, 3)
    taps = jnp.broadcast_to(taps, (8, 16, TILE, 512))
    p3, q3 = around_z(p2, 1), around_z(q2, -1)
    mine, cross = split_tokens(ids, [tokens, q1, p1, q2, p2])
    p4 = around_z(after(p3, own), 1)
    other = [to_other_core(block) for block in after(own, back, ahead, taps, mine)]
    acc, weight, mine, cross = project_own(ids, [q3, p3, p4], own, mine, cross)
    projected, tail, head, weight = project_other(ids, other, cross, acc, weight, d_gated)
    gated, d_proj, far, weight, cross = conv(
        ids, projected, tail, head, d_gated, taps, back, ahead, weight, cross
    )
    d_tokens, grad = sum_up(ids, d_proj, far, weight, mine, cross)
    return gated, d_tokens, grad * (1.0 / math.sqrt(seq_total))


def solution(mesh):
    placed = (P("row", "col"), P(), P("row", "col"), P(None, "col"), P("row", "col"))
    return jax.shard_map(
        body,
        mesh=mesh,
        in_specs=placed,
        out_specs=(P("row", "col"), P("row", "col"), P("row", "col")),
        check_vma=False,
    )
```

```python
import functools
import math

import jax
import jax.numpy as jnp
from jax import lax
from jax.experimental import pallas as pl
from jax.experimental.pallas import tpu as pltpu
from jax.sharding import PartitionSpec as P

BF = jnp.bfloat16
F32 = jnp.float32
NY, NX, NC, NZ = 4, 4, 2, 8
TILE = 16
LANES = 128


def row_of(y, x, c):
    return ((y % NY) * NX + x % NX) * NC + c % NC


CHIPS = [(y, x) for y in range(NY) for x in range(NX)]
def around_z(value, steps):
    pairs = []
    for y, x in CHIPS:
        for c in range(NC):
            for z in range(NZ):
                to = (z + steps * (1 - 2 * c)) % NZ
                pairs.append((row_of(y, x, c) * NZ + z, row_of(y, x, c) * NZ + to))
    return lax.ppermute(value, ("row", "col"), pairs)


def narrow(value, steps):
    pairs = []
    for y, x in CHIPS:
        pairs.append((row_of(y, x, 0), row_of(y, x + steps, 0)))
        pairs.append((row_of(y, x, 1), row_of(y + steps, x, 1)))
    return lax.ppermute(value, "row", pairs)


def wide(value, steps):
    pairs = []
    for y, x in CHIPS:
        pairs.append((row_of(y, x, 0), row_of(y + steps, x, 0)))
        pairs.append((row_of(y, x, 1), row_of(y, x + steps, 1)))
    return lax.ppermute(value, "row", pairs)


def to_other_core(value):
    return lax.ppermute(value, "row", [(row_of(y, x, c), row_of(y, x, c + 1)) for y, x in CHIPS for c in range(NC)])


def next_row(value, steps):
    count = NY * NX * NC
    return lax.ppermute(value, "row", [(r, (r + steps) % count) for r in range(count)])


def live_taps(contig_lengths, first_row, rows):
    ends = jnp.cumsum(contig_lengths)
    starts = ends - contig_lengths
    at = first_row + jnp.arange(rows, dtype=jnp.int32)
    start = jnp.max(jnp.where(starts[None, :] <= at[:, None], starts[None, :], 0), axis=1)
    end = jnp.min(jnp.where(ends[None, :] > at[:, None], ends[None, :], 1 << 30), axis=1)
    back = jnp.minimum(at - start, 127)
    ahead = jnp.minimum(end - 1 - at, 127)
    wide = lambda v: jnp.broadcast_to(v.astype(BF)[:, None], (rows, LANES))
    return wide(back), wide(ahead)


def after(value, *others):
    return lax.optimization_barrier((value, others))[0]


VMEM = pl.BlockSpec(memory_space=pltpu.VMEM)
SMEM = pl.BlockSpec(memory_space=pltpu.SMEM)
HBM = pl.BlockSpec(memory_space=pltpu.HBM)


def loop(count, step):
    def run(i, carry):
        step(i)
        return carry

    lax.fori_loop(jnp.int32(0), jnp.int32(count), run, jnp.int32(0))


def add_kernel(a, b, out):
    out[...] = (a[...].astype(F32) + b[...].astype(F32)).astype(BF)


def add(a, b):
    return pl.pallas_call(
        add_kernel,
        in_specs=[VMEM] * 2,
        out_specs=VMEM,
        out_shape=jax.ShapeDtypeStruct(a.shape, BF),
        compiler_params=pltpu.CompilerParams(vmem_limit_bytes=2 << 20),
        cost_estimate=pl.CostEstimate(flops=1 << 20, bytes_accessed=1 << 20, transcendentals=0),
        name="add",
    )(a, b)


def stack_kernel(first, *refs):
    for k in range(4):
        refs[4][lax.rem(first[0] + k, 4)] = refs[k][...]


def stack(first, pieces):
    return pl.pallas_call(
        stack_kernel,
        in_specs=[SMEM] + [VMEM] * 4,
        out_specs=VMEM,
        out_shape=jax.ShapeDtypeStruct((4, 128, 512), BF),
        compiler_params=pltpu.CompilerParams(vmem_limit_bytes=2 << 20),
        cost_estimate=pl.CostEstimate(flops=1 << 20, bytes_accessed=1 << 20, transcendentals=0),
        name="stack",
    )(first, *pieces)


def sum_kernel(*refs):
    for j in range(4):
        total = refs[0][j].astype(F32)
        for k in range(1, 4):
            total += refs[k][j].astype(F32)
        refs[4 + j][...] = total.astype(BF)


def sum_four(blocks):
    return pl.pallas_call(
        sum_kernel,
        in_specs=[VMEM] * 4,
        out_specs=[VMEM] * 4,
        out_shape=[jax.ShapeDtypeStruct((128, 512), BF)] * 4,
        compiler_params=pltpu.CompilerParams(vmem_limit_bytes=4 << 20),
        cost_estimate=pl.CostEstimate(flops=1 << 20, bytes_accessed=1 << 20, transcendentals=0),
        name="sum_four",
    )(*blocks)


def place_of(ids, steps):
    return lax.rem(ids[3] + jnp.where(ids[2] == 0, steps, NZ - steps), NZ)


def load_weight(ids, core, blocks, w, sems, act):
    @pl.when(core == 0)
    def _():
        for i, block in enumerate(blocks):
            act(pltpu.make_async_copy(block, w.at[lax.rem(ids[0] + i, 4), :, 0], sems.at[i]))

    @pl.when(core == 1)
    def _():
        for i, block in enumerate(blocks):
            act(pltpu.make_async_copy(block, w.at[:, lax.rem(ids[1] + i, 4), 1], sems.at[i]))


def weight_rows(ids, k, w):
    zb = place_of(ids, k)
    return w.at[zb // 2, pl.ds(lax.rem(zb, 2) * 2, 2)]


def start(copy):
    copy.start()


def wait(copy):
    copy.wait()


def start(copy):
    copy.start()


def wait(copy):
    copy.wait()


def split_piece(ids, k, piece, mine_ref, cross_ref):
    for core, out in ((ids[2], mine_ref), (1 - ids[2], cross_ref)):
        for xp in range(2):
            lanes = pl.ds(pl.multiple_of(xp * 256 + core * 128, 128), 128)
            out[k, :, xp * 128 : xp * 128 + 128] = piece[:, lanes]


FIRST, NEXT = (0, 1, 7, 2, 6), (3, 5, 4)


def split_kernel(ids, *refs):
    pieces, (mine_ref, cross_ref) = refs[0:5], refs[5:]
    for n, k in enumerate(FIRST):
        split_piece(ids, k, pieces[n], mine_ref, cross_ref)


def split_tokens(ids, pieces):
    return pl.pallas_call(
        split_kernel,
        in_specs=[SMEM] + [VMEM] * 5,
        out_specs=[VMEM] * 2,
        out_shape=[jax.ShapeDtypeStruct((n, 256, 256), BF) for n in (NZ, NZ + 2)],
        compiler_params=pltpu.CompilerParams(vmem_limit_bytes=4 << 20),
        cost_estimate=pl.CostEstimate(flops=1 << 20, bytes_accessed=4 << 20, transcendentals=0),
        name="split_tokens",
    )(ids, *pieces)


def core_term(ids, core, columns, w):
    total = None
    for k in range(NZ):
        rows = weight_rows(ids, k, w)[:, core].reshape(256, 512)
        term = jnp.dot(columns[k], rows, preferred_element_type=F32)
        total = term if total is None else total + term
    return total


def own_kernel(ids, *refs):
    pieces, own, (_, _, acc, w, mine_ref, cross_ref, sems) = refs[0:3], refs[3:7], refs[7:]
    load_weight(ids, ids[2], own, w, sems, start)
    for piece, k in zip(pieces, NEXT):
        split_piece(ids, k, piece, mine_ref, cross_ref)
    load_weight(ids, ids[2], own, w, sems, wait)
    acc[...] = core_term(ids, ids[2], mine_ref, w)


def project_own(ids, pieces, own, mine, cross):
    return pl.pallas_call(
        own_kernel,
        in_specs=[SMEM] + [VMEM] * 3 + [HBM] * 4 + [VMEM] * 2,
        out_specs=[VMEM] * 4,
        out_shape=[
            jax.ShapeDtypeStruct((256, 512), F32),
            jax.ShapeDtypeStruct((4, 4, 2, 128, 512), BF),
            jax.ShapeDtypeStruct(mine.shape, BF),
            jax.ShapeDtypeStruct(cross.shape, BF),
        ],
        input_output_aliases={8: 2, 9: 3},
        scratch_shapes=[pltpu.SemaphoreType.DMA((4,))],
        compiler_params=pltpu.CompilerParams(vmem_limit_bytes=6 << 20),
        cost_estimate=pl.CostEstimate(flops=1 << 32, bytes_accessed=4 << 20, transcendentals=0),
        name="project_own",
    )(ids, *pieces, *own, mine, cross)


def other_kernel(ids, *refs):
    other, (cross, acc, _, dg_ref, p_ref, tail_ref, head_ref, w, sems) = refs[0:4], refs[4:]
    load_weight(ids, 1 - ids[2], other, w, sems, start)
    load_weight(ids, 1 - ids[2], other, w, sems, wait)
    p = (acc[...] + core_term(ids, 1 - ids[2], cross, w)).astype(BF)
    p_ref[...] = p
    tail_ref[...] = p[128:256]
    top = p[0:128].astype(F32)
    head_ref[...] = (dg_ref[0:128].astype(F32) * (top * jax.nn.sigmoid(top))).astype(BF)


def project_other(ids, other, cross, acc, w, d_gated):
    half = jax.ShapeDtypeStruct((128, 512), BF)
    return pl.pallas_call(
        other_kernel,
        in_specs=[SMEM] + [HBM] * 4 + [VMEM] * 4,
        out_specs=[VMEM] * 4,
        out_shape=[jax.ShapeDtypeStruct((256, 512), BF), half, half, jax.ShapeDtypeStruct(w.shape, BF)],
        input_output_aliases={7: 3},
        scratch_shapes=[pltpu.SemaphoreType.DMA((4,))],
        compiler_params=pltpu.CompilerParams(vmem_limit_bytes=6 << 20),
        cost_estimate=pl.CostEstimate(flops=1 << 30, bytes_accessed=4 << 20, transcendentals=0),
        name="project_other",
    )(ids, *other, cross, acc, w, d_gated)


def mix(ext, live_ref, taps_ref, even, odd, acc, reverse):
    acc[...] = jnp.zeros_like(acc)
    rows = ext.shape[0]
    zero, one = jnp.zeros((), BF), jnp.ones((), BF)

    def shift(b):
        r = ext[...]
        even[...] = r.astype(BF)
        odd[...] = jnp.concatenate([r[8:], r[:8]] if reverse else [r[-8:], r[:-8]], 0).astype(BF)
        ext[...] = pltpu.roll(r, rows - 1 if reverse else 1, 0)
        for u in range(8):
            at = slice(TILE * u, TILE * u + TILE)
            live = live_ref[at] - b.astype(F32).astype(BF)
            sums = []
            for k in range(16):
                v = u + k // 2 if reverse else u + 8 - k // 2
                source = (odd if k % 2 else even)[TILE * v : TILE * v + TILE]
                m = jnp.minimum(jnp.maximum(live - jnp.array(8 * k - 1, BF), zero), one)
                term = source * taps_ref[b, k] * jnp.concatenate([m] * 4, 1)
                level = k
                while level % 2:
                    term = sums.pop() + term
                    level //= 2
                sums.append(term)
            acc[at] += sums[0].astype(F32)

    loop(8, shift)


def gates(p, up, out):
    sigma = jax.nn.sigmoid(p)
    gate = p * sigma
    return (out * gate).astype(BF), up * out * (sigma * (1.0 + p * (1.0 - sigma))), up * gate


LOW, HIGH = slice(0, 128), slice(128, 256)


def inside_kernel(
    p_ref, dg_ref, taps_ref, back_ref, ahead_ref, gated_ref, dgate_ref, part_ref, dconv_ref, ext, even, odd, acc
):
    ext[...] = p_ref[...].astype(F32)
    mix(ext, back_ref.at[HIGH], taps_ref, even, odd, acc, False)
    p, up = p_ref[HIGH].astype(F32), dg_ref[HIGH].astype(F32)
    gated_ref[...], dgate_ref[...], ext[HIGH] = gates(p, up, acc[...])
    p, up = p_ref[LOW].astype(F32), dg_ref[LOW].astype(F32)
    ext[LOW] = up * (p * jax.nn.sigmoid(p))
    dconv_ref[...] = ext[HIGH]
    mix(ext, ahead_ref.at[LOW], taps_ref, even, odd, part_ref, True)


def edges_kernel(
    p_ref, dg_ref, taps_ref, back_ref, ahead_ref, tail_ref, head_ref, gated_hi, dgate_ref, part_ref, dconv_ref,
    ids, w_ref, _, gated_ref, dproj_ref, far_ref, w, cross_ref, ext, even, odd, acc, sem,
):
    load = pltpu.make_async_copy(w_ref, w, sem)
    load.start()
    p, up = p_ref[LOW].astype(F32), dg_ref[LOW].astype(F32)
    ext[LOW] = tail_ref[...].astype(F32)
    ext[HIGH] = p
    mix(ext, back_ref.at[LOW], taps_ref, even, odd, acc, False)
    gated_ref[LOW], d_gate, _ = gates(p, up, acc[...])
    gated_ref[HIGH] = gated_hi[...]
    dproj_ref[LOW] = (part_ref[...] + d_gate).astype(BF)
    ext[LOW] = dconv_ref[...]
    ext[HIGH] = head_ref[...].astype(F32)
    mix(ext, ahead_ref.at[HIGH], taps_ref, even, odd, acc, True)
    dproj_ref[HIGH] = (acc[...] + dgate_ref[...]).astype(BF)
    cross_ref[NZ] = dproj_ref[:, 0:256]
    cross_ref[NZ + 1] = dproj_ref[:, 256:512]
    load.wait()
    far_ref[...] = back_term(dproj_ref[...], weight_rows(ids, 4, w)[...].reshape(512, 512))


def back_term(d, block):
    return lax.dot_general(d, block, (((1,), (1,)), ((), ())), preferred_element_type=F32).astype(BF)


def mix_call(kernel, name, shapes, *operands, specs=None, scratch=(), aliases={}):
    return pl.pallas_call(
        kernel,
        in_specs=specs or [VMEM] * len(operands),
        out_specs=[VMEM] * len(shapes),
        out_shape=[jax.ShapeDtypeStruct(shape, kind) for shape, kind in shapes],
        scratch_shapes=[
            pltpu.VMEM((256, 512), F32),
            pltpu.VMEM((256, 512), BF),
            pltpu.VMEM((256, 512), BF),
            pltpu.VMEM((128, 512), F32),
            *scratch,
        ],
        input_output_aliases=aliases,
        compiler_params=pltpu.CompilerParams(vmem_limit_bytes=8 << 20),
        cost_estimate=pl.CostEstimate(flops=1 << 32, bytes_accessed=4 << 20, transcendentals=0),
        name=name,
    )(*operands)


def conv(ids, p, tail, head, d_gated, taps, back, ahead, w, cross):
    half, whole = (128, 512), (256, 512)
    tail, head = next_row(tail, 1), next_row(head, -1)
    inside = mix_call(
        inside_kernel, "inside", [(half, BF), (half, F32), (half, F32), (half, F32)], p, d_gated, taps, back, ahead
    )
    return mix_call(
        edges_kernel, "edges", [(whole, BF), (whole, BF), (whole, BF), (w.shape, BF), (cross.shape, BF)],
        p, d_gated, taps, back, ahead, tail, head, *inside, ids, w, cross,
        specs=[VMEM] * 11 + [SMEM, HBM, VMEM], scratch=[pltpu.SemaphoreType.DMA], aliases={13: 4},
    )


NEAR = (3, 5, 2, 6, 1, 7, 0)


def near_kernel(ids, d_ref, w, *outs):
    d = d_ref[...]
    for steps, out in zip(NEAR, outs):
        out[...] = back_term(d, weight_rows(ids, steps, w)[...].reshape(512, 512))


def near_terms(ids, d_proj, weight):
    return pl.pallas_call(
        near_kernel,
        in_specs=[SMEM, VMEM, VMEM],
        out_specs=[VMEM] * 7,
        out_shape=[jax.ShapeDtypeStruct((256, 512), BF)] * 7,
        compiler_params=pltpu.CompilerParams(vmem_limit_bytes=4 << 20),
        cost_estimate=pl.CostEstimate(flops=2 * 256 * 512 * 512 * 7, bytes_accessed=6 << 20, transcendentals=0),
        name="near_terms",
    )(ids, d_proj, weight)


def add_three_kernel(a, b, c, out):
    out[...] = (a[...].astype(F32) + b[...].astype(F32) + c[...].astype(F32)).astype(BF)


def add_three(a, b, c):
    return pl.pallas_call(
        add_three_kernel,
        in_specs=[VMEM] * 3,
        out_specs=VMEM,
        out_shape=jax.ShapeDtypeStruct(a.shape, BF),
        compiler_params=pltpu.CompilerParams(vmem_limit_bytes=2 << 20),
        cost_estimate=pl.CostEstimate(flops=1 << 34, bytes_accessed=1 << 20, transcendentals=0),
        name="add_three",
    )(a, b, c)


def grad_kernel(ids, mine, theirs, d_mine, *refs):
    outs, out, d_theirs = refs[:4], refs[4], refs[5]
    d_theirs[:, 0:256] = theirs[NZ]
    d_theirs[:, 256:512] = theirs[NZ + 1]
    me = ids[2]
    dims = (((0,), (0,)), ((), ()))
    for k in range(NZ):
        zb = place_of(ids, k)
        total = lax.dot_general(mine[k], d_mine[...], dims, preferred_element_type=F32)
        total += lax.dot_general(theirs[(NZ - k) % NZ], d_theirs[...], dims, preferred_element_type=F32)
        total = total.astype(BF)
        for xp in range(2):
            dy = lax.rem(zb // 2 + 4 - ids[0], 4)
            dx = lax.rem(lax.rem(zb, 2) * 2 + xp + 4 - ids[1], 4)
            out[jnp.where(me == 0, dy, dx), jnp.where(me == 0, dx, dy)] = total[xp * 128 : xp * 128 + 128]
    for k in range(4):
        outs[k][...] = out[k]


def weight_terms(ids, mine, theirs, d_mine):
    return pl.pallas_call(
        grad_kernel,
        in_specs=[SMEM] + [VMEM] * 3,
        out_specs=[VMEM] * 4,
        out_shape=[jax.ShapeDtypeStruct((4, 128, 512), BF)] * 4,
        scratch_shapes=[pltpu.VMEM((4, 4, 128, 512), BF), pltpu.VMEM((256, 512), BF)],
        compiler_params=pltpu.CompilerParams(vmem_limit_bytes=6 << 20),
        cost_estimate=pl.CostEstimate(flops=2 * 512 * 2048 * 512, bytes_accessed=5 << 20, transcendentals=0),
        name="weight_terms",
    )(ids, mine, theirs, d_mine)


def sum_up(ids, d_proj, far, weight, mine, cross):
    p = around_z(far, 1)
    theirs = to_other_core(cross)
    p3, q3, p2, q2, p1, q1, own = near_terms(ids, d_proj, weight)
    q = around_z(q3, -1)
    g = weight_terms(ids, mine, after(theirs, own), d_proj)
    p = around_z(add(after(p3, g[0]), p), 1)
    s = [g[0]] + [wide(g[k], k) for k in (1, 2, 3)]
    q = around_z(add(q2, q), -1)
    p = around_z(add(p2, p), 1)
    q_last = add(q1, q)
    q = around_z(q_last, -1)
    p_last = add(p1, p)
    p = around_z(p_last, 1)
    n = sum_four([after(s[0], p_last, q_last)] + s[1:])
    n = [n[0]] + [narrow(n[k], k) for k in (1, 2, 3)]
    d_tokens = add_three(own, p, q)
    return d_tokens, sum(v.astype(F32) for v in after(n, d_tokens))


def body(tokens, contig_lengths, w_in, conv_filter, d_gated):
    rows = tokens.shape[0]
    seq_total = rows * NY * NX * NC
    row, z = lax.axis_index("row"), lax.axis_index("col")
    core, chip = row % NC, row // NC
    y, x = chip // NX, chip % NX
    ids = jnp.stack([y, x, core, z]).astype(jnp.int32)

    w = [narrow(w_in, 4 - k) for k in (1, 2, 3)]
    p1, q1 = around_z(tokens, 1), around_z(tokens, -1)
    first = jnp.where(core == 0, x, y).astype(jnp.int32).reshape(1)
    row_block = stack(first, [w_in] + w)
    own = [row_block] + [wide(row_block, 4 - k) for k in (1, 2, 3)]
    p2, q2 = around_z(after(p1, row_block), 1), around_z(after(q1, row_block), -1)
    conv_filter, contig_lengths = after((conv_filter, contig_lengths), q1)
    back, ahead = live_taps(contig_lengths, row * rows, rows)
    taps = conv_filter.astype(BF).reshape(16, 8, 1, 512).transpose(1, 0, 2, 3)
    taps = jnp.broadcast_to(taps, (8, 16, TILE, 512))
    p3, q3 = around_z(p2, 1), around_z(q2, -1)
    mine, cross = split_tokens(ids, [tokens, q1, p1, q2, p2])
    p4 = around_z(after(p3, own), 1)
    other = [to_other_core(block) for block in after(own, back, ahead, taps, mine)]
    acc, weight, mine, cross = project_own(ids, [q3, p3, p4], own, mine, cross)
    projected, tail, head, weight = project_other(ids, other, cross, acc, weight, d_gated)
    gated, d_proj, far, weight, cross = conv(
        ids, projected, tail, head, d_gated, taps, back, ahead, weight, cross
    )
    d_tokens, grad = sum_up(ids, d_proj, far, weight, mine, cross)
    return gated, d_tokens, grad * (1.0 / math.sqrt(seq_total))


def solution(mesh):
    placed = (P("row", "col"), P(), P("row", "col"), P(None, "col"), P("row", "col"))
    return jax.shard_map(
        body,
        mesh=mesh,
        in_specs=placed,
        out_specs=(P("row", "col"), P("row", "col"), P("row", "col")),
        check_vma=False,
    )
```

```python
import functools
import math

import jax
import jax.numpy as jnp
from jax import lax
from jax.experimental import pallas as pl
from jax.experimental.pallas import tpu as pltpu
from jax.sharding import PartitionSpec as P

BF = jnp.bfloat16
F32 = jnp.float32
NY, NX, NC, NZ = 4, 4, 2, 8
TILE = 16
LANES = 128


def row_of(y, x, c):
    return ((y % NY) * NX + x % NX) * NC + c % NC


CHIPS = [(y, x) for y in range(NY) for x in range(NX)]
def around_z(value, steps):
    pairs = []
    for y, x in CHIPS:
        for c in range(NC):
            for z in range(NZ):
                to = (z + steps * (1 - 2 * c)) % NZ
                pairs.append((row_of(y, x, c) * NZ + z, row_of(y, x, c) * NZ + to))
    return lax.ppermute(value, ("row", "col"), pairs)


def narrow(value, steps):
    pairs = []
    for y, x in CHIPS:
        pairs.append((row_of(y, x, 0), row_of(y, x + steps, 0)))
        pairs.append((row_of(y, x, 1), row_of(y + steps, x, 1)))
    return lax.ppermute(value, "row", pairs)


def wide(value, steps):
    pairs = []
    for y, x in CHIPS:
        pairs.append((row_of(y, x, 0), row_of(y + steps, x, 0)))
        pairs.append((row_of(y, x, 1), row_of(y, x + steps, 1)))
    return lax.ppermute(value, "row", pairs)


def to_other_core(value):
    return lax.ppermute(value, "row", [(row_of(y, x, c), row_of(y, x, c + 1)) for y, x in CHIPS for c in range(NC)])


def to_next_chip(value):
    count = NY * NX * NC
    pairs = [(r, (r + 1) % count) for r in range(1, count, 2)] + [(r, (r - 1) % count) for r in range(0, count, 2)]
    return lax.ppermute(value, "row", pairs)


def live_taps(contig_lengths, first_row, rows):
    ends = jnp.cumsum(contig_lengths)
    starts = ends - contig_lengths
    at = first_row + jnp.arange(rows, dtype=jnp.int32)
    start = jnp.max(jnp.where(starts[None, :] <= at[:, None], starts[None, :], 0), axis=1)
    end = jnp.min(jnp.where(ends[None, :] > at[:, None], ends[None, :], 1 << 30), axis=1)
    back = jnp.minimum(at - start, 127)
    ahead = jnp.minimum(end - 1 - at, 127)
    wide = lambda v: jnp.broadcast_to(v.astype(BF)[:, None], (rows, LANES))
    return wide(back), wide(ahead)


def after(value, *others):
    return lax.optimization_barrier((value, others))[0]


VMEM = pl.BlockSpec(memory_space=pltpu.VMEM)
SMEM = pl.BlockSpec(memory_space=pltpu.SMEM)
HBM = pl.BlockSpec(memory_space=pltpu.HBM)


def loop(count, step):
    def run(i, carry):
        step(i)
        return carry

    lax.fori_loop(jnp.int32(0), jnp.int32(count), run, jnp.int32(0))


def add_kernel(a, b, out):
    out[...] = (a[...].astype(F32) + b[...].astype(F32)).astype(BF)


def add(a, b):
    return pl.pallas_call(
        add_kernel,
        in_specs=[VMEM] * 2,
        out_specs=VMEM,
        out_shape=jax.ShapeDtypeStruct(a.shape, BF),
        compiler_params=pltpu.CompilerParams(vmem_limit_bytes=2 << 20),
        cost_estimate=pl.CostEstimate(flops=1 << 20, bytes_accessed=1 << 20, transcendentals=0),
        name="add",
    )(a, b)


def stack_kernel(first, *refs):
    for k in range(4):
        refs[4][lax.rem(first[0] + k, 4)] = refs[k][...]


def stack(first, pieces):
    return pl.pallas_call(
        stack_kernel,
        in_specs=[SMEM] + [VMEM] * 4,
        out_specs=VMEM,
        out_shape=jax.ShapeDtypeStruct((4, 128, 512), BF),
        compiler_params=pltpu.CompilerParams(vmem_limit_bytes=2 << 20),
        cost_estimate=pl.CostEstimate(flops=1 << 20, bytes_accessed=1 << 20, transcendentals=0),
        name="stack",
    )(first, *pieces)


def sum_kernel(*refs):
    for j in range(4):
        total = refs[0][j].astype(F32)
        for k in range(1, 4):
            total += refs[k][j].astype(F32)
        refs[4 + j][...] = total.astype(BF)


def sum_four(blocks):
    return pl.pallas_call(
        sum_kernel,
        in_specs=[VMEM] * 4,
        out_specs=[VMEM] * 4,
        out_shape=[jax.ShapeDtypeStruct((128, 512), BF)] * 4,
        compiler_params=pltpu.CompilerParams(vmem_limit_bytes=4 << 20),
        cost_estimate=pl.CostEstimate(flops=1 << 20, bytes_accessed=1 << 20, transcendentals=0),
        name="sum_four",
    )(*blocks)


def place_of(ids, steps):
    return lax.rem(ids[3] + jnp.where(ids[2] == 0, steps, NZ - steps), NZ)


def load_weight(ids, core, blocks, w, sems, act):
    @pl.when(core == 0)
    def _():
        for i, block in enumerate(blocks):
            act(pltpu.make_async_copy(block, w.at[lax.rem(ids[0] + i, 4), :, 0], sems.at[i]))

    @pl.when(core == 1)
    def _():
        for i, block in enumerate(blocks):
            act(pltpu.make_async_copy(block, w.at[:, lax.rem(ids[1] + i, 4), 1], sems.at[i]))


def weight_rows(ids, k, w):
    zb = place_of(ids, k)
    return w.at[zb // 2, pl.ds(lax.rem(zb, 2) * 2, 2)]


def start(copy):
    copy.start()


def wait(copy):
    copy.wait()


def start(copy):
    copy.start()


def wait(copy):
    copy.wait()


def split_piece(ids, k, piece, mine_ref, cross_ref):
    for core, out in ((ids[2], mine_ref), (1 - ids[2], cross_ref)):
        for xp in range(2):
            lanes = pl.ds(pl.multiple_of(xp * 256 + core * 128, 128), 128)
            out[k, :, xp * 128 : xp * 128 + 128] = piece[:, lanes]


FIRST, NEXT = (0, 1, 7, 2, 6), (3, 5, 4)


def split_kernel(ids, *refs):
    pieces, (mine_ref, cross_ref) = refs[0:5], refs[5:]
    for n, k in enumerate(FIRST):
        split_piece(ids, k, pieces[n], mine_ref, cross_ref)


def split_tokens(ids, pieces):
    return pl.pallas_call(
        split_kernel,
        in_specs=[SMEM] + [VMEM] * 5,
        out_specs=[VMEM] * 2,
        out_shape=[jax.ShapeDtypeStruct((n, 256, 256), BF) for n in (NZ, NZ + 2)],
        compiler_params=pltpu.CompilerParams(vmem_limit_bytes=4 << 20),
        cost_estimate=pl.CostEstimate(flops=1 << 20, bytes_accessed=4 << 20, transcendentals=0),
        name="split_tokens",
    )(ids, *pieces)


def core_term(ids, core, columns, w):
    total = None
    for k in range(NZ):
        rows = weight_rows(ids, k, w)[:, core].reshape(256, 512)
        term = jnp.dot(columns[k], rows, preferred_element_type=F32)
        total = term if total is None else total + term
    return total


def own_kernel(ids, *refs):
    pieces, own, (_, _, acc, w, mine_ref, cross_ref, sems) = refs[0:3], refs[3:7], refs[7:]
    load_weight(ids, ids[2], own, w, sems, start)
    for piece, k in zip(pieces, NEXT):
        split_piece(ids, k, piece, mine_ref, cross_ref)
    load_weight(ids, ids[2], own, w, sems, wait)
    acc[...] = core_term(ids, ids[2], mine_ref, w)


def project_own(ids, pieces, own, mine, cross):
    return pl.pallas_call(
        own_kernel,
        in_specs=[SMEM] + [VMEM] * 3 + [HBM] * 4 + [VMEM] * 2,
        out_specs=[VMEM] * 4,
        out_shape=[
            jax.ShapeDtypeStruct((256, 512), F32),
            jax.ShapeDtypeStruct((4, 4, 2, 128, 512), BF),
            jax.ShapeDtypeStruct(mine.shape, BF),
            jax.ShapeDtypeStruct(cross.shape, BF),
        ],
        input_output_aliases={8: 2, 9: 3},
        scratch_shapes=[pltpu.SemaphoreType.DMA((4,))],
        compiler_params=pltpu.CompilerParams(vmem_limit_bytes=6 << 20),
        cost_estimate=pl.CostEstimate(flops=1 << 32, bytes_accessed=4 << 20, transcendentals=0),
        name="project_own",
    )(ids, *pieces, *own, mine, cross)


def other_kernel(ids, *refs):
    other, (cross, acc, _, dg_ref, p_ref, chip_ref, next_ref, w, sems) = refs[0:4], refs[4:]
    load_weight(ids, 1 - ids[2], other, w, sems, start)
    load_weight(ids, 1 - ids[2], other, w, sems, wait)
    p = (acc[...] + core_term(ids, 1 - ids[2], cross, w)).astype(BF)
    p_ref[...] = p
    tail = p[128:256]
    top = p[0:128].astype(F32)
    head = (dg_ref[0:128].astype(F32) * (top * jax.nn.sigmoid(top))).astype(BF)

    @pl.when(ids[2] == 0)
    def _():
        chip_ref[...], next_ref[...] = tail, head

    @pl.when(ids[2] == 1)
    def _():
        chip_ref[...], next_ref[...] = head, tail


def project_other(ids, other, cross, acc, w, d_gated):
    half = jax.ShapeDtypeStruct((128, 512), BF)
    return pl.pallas_call(
        other_kernel,
        in_specs=[SMEM] + [HBM] * 4 + [VMEM] * 4,
        out_specs=[VMEM] * 4,
        out_shape=[jax.ShapeDtypeStruct((256, 512), BF), half, half, jax.ShapeDtypeStruct(w.shape, BF)],
        input_output_aliases={7: 3},
        scratch_shapes=[pltpu.SemaphoreType.DMA((4,))],
        compiler_params=pltpu.CompilerParams(vmem_limit_bytes=6 << 20),
        cost_estimate=pl.CostEstimate(flops=1 << 30, bytes_accessed=4 << 20, transcendentals=0),
        name="project_other",
    )(ids, *other, cross, acc, w, d_gated)


def mix(ext, live_ref, taps_ref, even, odd, acc, reverse):
    acc[...] = jnp.zeros_like(acc)
    rows = ext.shape[0]
    zero, one = jnp.zeros((), BF), jnp.ones((), BF)

    def shift(b):
        r = ext[...]
        even[...] = r.astype(BF)
        odd[...] = jnp.concatenate([r[8:], r[:8]] if reverse else [r[-8:], r[:-8]], 0).astype(BF)
        ext[...] = pltpu.roll(r, rows - 1 if reverse else 1, 0)
        for u in range(8):
            at = slice(TILE * u, TILE * u + TILE)
            live = live_ref[at] - b.astype(F32).astype(BF)
            sums = []
            for k in range(16):
                v = u + k // 2 if reverse else u + 8 - k // 2
                source = (odd if k % 2 else even)[TILE * v : TILE * v + TILE]
                m = jnp.minimum(jnp.maximum(live - jnp.array(8 * k - 1, BF), zero), one)
                term = source * taps_ref[b, k] * jnp.concatenate([m] * 4, 1)
                level = k
                while level % 2:
                    term = sums.pop() + term
                    level //= 2
                sums.append(term)
            acc[at] += sums[0].astype(F32)

    loop(8, shift)


def gates(p, up, out):
    sigma = jax.nn.sigmoid(p)
    gate = p * sigma
    return (out * gate).astype(BF), up * out * (sigma * (1.0 + p * (1.0 - sigma))), up * gate


LOW, HIGH = slice(0, 128), slice(128, 256)


def inside_kernel(
    p_ref, dg_ref, taps_ref, back_ref, ahead_ref, gated_ref, dgate_ref, part_ref, dconv_ref, ext, even, odd, acc
):
    ext[...] = p_ref[...].astype(F32)
    mix(ext, back_ref.at[HIGH], taps_ref, even, odd, acc, False)
    p, up = p_ref[HIGH].astype(F32), dg_ref[HIGH].astype(F32)
    gated_ref[...], dgate_ref[...], ext[HIGH] = gates(p, up, acc[...])
    p, up = p_ref[LOW].astype(F32), dg_ref[LOW].astype(F32)
    ext[LOW] = up * (p * jax.nn.sigmoid(p))
    dconv_ref[...] = ext[HIGH]
    mix(ext, ahead_ref.at[LOW], taps_ref, even, odd, part_ref, True)


def edges_kernel(
    p_ref, dg_ref, taps_ref, back_ref, ahead_ref, chip_ref, next_ref, gated_hi, dgate_ref, part_ref, dconv_ref,
    ids, w_ref, _, gated_ref, dproj_ref, far_ref, w, cross_ref, ext, even, odd, acc, sem,
):
    load = pltpu.make_async_copy(w_ref, w, sem)
    load.start()
    p, up = p_ref[LOW].astype(F32), dg_ref[LOW].astype(F32)
    from_chip, from_next = chip_ref[...].astype(F32), next_ref[...].astype(F32)
    ext[LOW] = jnp.where(ids[2] == 0, from_next, from_chip)
    ext[HIGH] = p
    mix(ext, back_ref.at[LOW], taps_ref, even, odd, acc, False)
    gated_ref[LOW], d_gate, _ = gates(p, up, acc[...])
    gated_ref[HIGH] = gated_hi[...]
    dproj_ref[LOW] = (part_ref[...] + d_gate).astype(BF)
    ext[LOW] = dconv_ref[...]
    from_chip, from_next = chip_ref[...].astype(F32), next_ref[...].astype(F32)
    ext[HIGH] = jnp.where(ids[2] == 0, from_chip, from_next)
    mix(ext, ahead_ref.at[HIGH], taps_ref, even, odd, acc, True)
    dproj_ref[HIGH] = (acc[...] + dgate_ref[...]).astype(BF)
    cross_ref[NZ] = dproj_ref[:, 0:256]
    cross_ref[NZ + 1] = dproj_ref[:, 256:512]
    load.wait()
    far_ref[...] = back_term(dproj_ref[...], weight_rows(ids, 4, w)[...].reshape(512, 512))


def back_term(d, block):
    return lax.dot_general(d, block, (((1,), (1,)), ((), ())), preferred_element_type=F32).astype(BF)


def mix_call(kernel, name, shapes, *operands, specs=None, scratch=(), aliases={}):
    return pl.pallas_call(
        kernel,
        in_specs=specs or [VMEM] * len(operands),
        out_specs=[VMEM] * len(shapes),
        out_shape=[jax.ShapeDtypeStruct(shape, kind) for shape, kind in shapes],
        scratch_shapes=[
            pltpu.VMEM((256, 512), F32),
            pltpu.VMEM((256, 512), BF),
            pltpu.VMEM((256, 512), BF),
            pltpu.VMEM((128, 512), F32),
            *scratch,
        ],
        input_output_aliases=aliases,
        compiler_params=pltpu.CompilerParams(vmem_limit_bytes=8 << 20),
        cost_estimate=pl.CostEstimate(flops=1 << 32, bytes_accessed=4 << 20, transcendentals=0),
        name=name,
    )(*operands)


def conv(ids, p, for_chip, for_next, d_gated, taps, back, ahead, w, cross):
    half, whole = (128, 512), (256, 512)
    halos = to_other_core(for_chip), to_next_chip(for_next)
    inside = mix_call(
        inside_kernel, "inside", [(half, BF), (half, F32), (half, F32), (half, F32)], p, d_gated, taps, back, ahead
    )
    return mix_call(
        edges_kernel, "edges", [(whole, BF), (whole, BF), (whole, BF), (w.shape, BF), (cross.shape, BF)],
        p, d_gated, taps, back, ahead, *halos, *inside, ids, w, cross,
        specs=[VMEM] * 11 + [SMEM, HBM, VMEM], scratch=[pltpu.SemaphoreType.DMA], aliases={13: 4},
    )


NEAR = (3, 5, 2, 6, 1, 7, 0)


def near_kernel(ids, d_ref, w, *outs):
    d = d_ref[...]
    for steps, out in zip(NEAR, outs):
        out[...] = back_term(d, weight_rows(ids, steps, w)[...].reshape(512, 512))


def near_terms(ids, d_proj, weight):
    return pl.pallas_call(
        near_kernel,
        in_specs=[SMEM, VMEM, VMEM],
        out_specs=[VMEM] * 7,
        out_shape=[jax.ShapeDtypeStruct((256, 512), BF)] * 7,
        compiler_params=pltpu.CompilerParams(vmem_limit_bytes=4 << 20),
        cost_estimate=pl.CostEstimate(flops=2 * 256 * 512 * 512 * 7, bytes_accessed=6 << 20, transcendentals=0),
        name="near_terms",
    )(ids, d_proj, weight)


def add_three_kernel(a, b, c, out):
    out[...] = (a[...].astype(F32) + b[...].astype(F32) + c[...].astype(F32)).astype(BF)


def add_three(a, b, c):
    return pl.pallas_call(
        add_three_kernel,
        in_specs=[VMEM] * 3,
        out_specs=VMEM,
        out_shape=jax.ShapeDtypeStruct(a.shape, BF),
        compiler_params=pltpu.CompilerParams(vmem_limit_bytes=2 << 20),
        cost_estimate=pl.CostEstimate(flops=1 << 34, bytes_accessed=1 << 20, transcendentals=0),
        name="add_three",
    )(a, b, c)


def grad_kernel(ids, mine, theirs, d_mine, *refs):
    outs, out, d_theirs = refs[:4], refs[4], refs[5]
    d_theirs[:, 0:256] = theirs[NZ]
    d_theirs[:, 256:512] = theirs[NZ + 1]
    me = ids[2]
    dims = (((0,), (0,)), ((), ()))
    for k in range(NZ):
        zb = place_of(ids, k)
        total = lax.dot_general(mine[k], d_mine[...], dims, preferred_element_type=F32)
        total += lax.dot_general(theirs[(NZ - k) % NZ], d_theirs[...], dims, preferred_element_type=F32)
        total = total.astype(BF)
        for xp in range(2):
            dy = lax.rem(zb // 2 + 4 - ids[0], 4)
            dx = lax.rem(lax.rem(zb, 2) * 2 + xp + 4 - ids[1], 4)
            out[jnp.where(me == 0, dy, dx), jnp.where(me == 0, dx, dy)] = total[xp * 128 : xp * 128 + 128]
    for k in range(4):
        outs[k][...] = out[k]


def weight_terms(ids, mine, theirs, d_mine):
    return pl.pallas_call(
        grad_kernel,
        in_specs=[SMEM] + [VMEM] * 3,
        out_specs=[VMEM] * 4,
        out_shape=[jax.ShapeDtypeStruct((4, 128, 512), BF)] * 4,
        scratch_shapes=[pltpu.VMEM((4, 4, 128, 512), BF), pltpu.VMEM((256, 512), BF)],
        compiler_params=pltpu.CompilerParams(vmem_limit_bytes=6 << 20),
        cost_estimate=pl.CostEstimate(flops=2 * 512 * 2048 * 512, bytes_accessed=5 << 20, transcendentals=0),
        name="weight_terms",
    )(ids, mine, theirs, d_mine)


def sum_up(ids, d_proj, far, weight, mine, cross):
    p = around_z(far, 1)
    theirs = to_other_core(cross)
    p3, q3, p2, q2, p1, q1, own = near_terms(ids, d_proj, weight)
    q = around_z(q3, -1)
    g = weight_terms(ids, mine, after(theirs, own), d_proj)
    p = around_z(add(after(p3, g[0]), p), 1)
    s = [g[0]] + [wide(g[k], k) for k in (1, 2, 3)]
    q = around_z(add(q2, q), -1)
    p = around_z(add(p2, p), 1)
    q_last = add(q1, q)
    q = around_z(q_last, -1)
    p_last = add(p1, p)
    p = around_z(p_last, 1)
    n = sum_four([after(s[0], p_last, q_last)] + s[1:])
    n = [n[0]] + [narrow(n[k], k) for k in (1, 2, 3)]
    d_tokens = add_three(own, p, q)
    return d_tokens, sum(v.astype(F32) for v in after(n, d_tokens))


def body(tokens, contig_lengths, w_in, conv_filter, d_gated):
    rows = tokens.shape[0]
    seq_total = rows * NY * NX * NC
    row, z = lax.axis_index("row"), lax.axis_index("col")
    core, chip = row % NC, row // NC
    y, x = chip // NX, chip % NX
    ids = jnp.stack([y, x, core, z]).astype(jnp.int32)

    w = [narrow(w_in, 4 - k) for k in (1, 2, 3)]
    p1, q1 = around_z(tokens, 1), around_z(tokens, -1)
    first = jnp.where(core == 0, x, y).astype(jnp.int32).reshape(1)
    row_block = stack(first, [w_in] + w)
    own = [row_block] + [wide(row_block, 4 - k) for k in (1, 2, 3)]
    p2, q2 = around_z(after(p1, row_block), 1), around_z(after(q1, row_block), -1)
    conv_filter, contig_lengths = after((conv_filter, contig_lengths), q1)
    back, ahead = live_taps(contig_lengths, row * rows, rows)
    taps = conv_filter.astype(BF).reshape(16, 8, 1, 512).transpose(1, 0, 2, 3)
    taps = jnp.broadcast_to(taps, (8, 16, TILE, 512))
    p3, q3 = around_z(p2, 1), around_z(q2, -1)
    mine, cross = split_tokens(ids, [tokens, q1, p1, q2, p2])
    p4 = around_z(after(p3, own), 1)
    other = [to_other_core(block) for block in after(own, back, ahead, taps, mine)]
    acc, weight, mine, cross = project_own(ids, [q3, p3, p4], own, mine, cross)
    projected, for_chip, for_next, weight = project_other(ids, other, cross, acc, weight, d_gated)
    gated, d_proj, far, weight, cross = conv(
        ids, projected, for_chip, for_next, d_gated, taps, back, ahead, weight, cross
    )
    d_tokens, grad = sum_up(ids, d_proj, far, weight, mine, cross)
    return gated, d_tokens, grad * (1.0 / math.sqrt(seq_total))


def solution(mesh):
    placed = (P("row", "col"), P(), P("row", "col"), P(None, "col"), P("row", "col"))
    return jax.shard_map(
        body,
        mesh=mesh,
        in_specs=placed,
        out_specs=(P("row", "col"), P("row", "col"), P("row", "col")),
        check_vma=False,
    )
```

```python
import functools
import math

import jax
import jax.numpy as jnp
from jax import lax
from jax.experimental import pallas as pl
from jax.experimental.pallas import tpu as pltpu
from jax.sharding import PartitionSpec as P

BF = jnp.bfloat16
F32 = jnp.float32
NY, NX, NC, NZ = 4, 4, 2, 8
TILE = 16
LANES = 128


def row_of(y, x, c):
    return ((y % NY) * NX + x % NX) * NC + c % NC


CHIPS = [(y, x) for y in range(NY) for x in range(NX)]
def around_z(value, steps):
    pairs = []
    for y, x in CHIPS:
        for c in range(NC):
            for z in range(NZ):
                to = (z + steps * (1 - 2 * c)) % NZ
                pairs.append((row_of(y, x, c) * NZ + z, row_of(y, x, c) * NZ + to))
    return lax.ppermute(value, ("row", "col"), pairs)


def narrow(value, steps):
    pairs = []
    for y, x in CHIPS:
        pairs.append((row_of(y, x, 0), row_of(y, x + steps, 0)))
        pairs.append((row_of(y, x, 1), row_of(y + steps, x, 1)))
    return lax.ppermute(value, "row", pairs)


def wide(value, steps):
    pairs = []
    for y, x in CHIPS:
        pairs.append((row_of(y, x, 0), row_of(y + steps, x, 0)))
        pairs.append((row_of(y, x, 1), row_of(y, x + steps, 1)))
    return lax.ppermute(value, "row", pairs)


def to_other_core(value):
    return lax.ppermute(value, "row", [(row_of(y, x, c), row_of(y, x, c + 1)) for y, x in CHIPS for c in range(NC)])


def to_next_chip(value):
    count = NY * NX * NC
    pairs = [(r, (r + 1) % count) for r in range(1, count, 2)] + [(r, (r - 1) % count) for r in range(0, count, 2)]
    return lax.ppermute(value, "row", pairs)


def live_taps(contig_lengths, first_row, rows):
    ends = jnp.cumsum(contig_lengths)
    starts = ends - contig_lengths
    at = first_row + jnp.arange(rows, dtype=jnp.int32)
    start = jnp.max(jnp.where(starts[None, :] <= at[:, None], starts[None, :], 0), axis=1)
    end = jnp.min(jnp.where(ends[None, :] > at[:, None], ends[None, :], 1 << 30), axis=1)
    back = jnp.minimum(at - start, 127)
    ahead = jnp.minimum(end - 1 - at, 127)
    wide = lambda v: jnp.broadcast_to(v.astype(BF)[:, None], (rows, LANES))
    return wide(back), wide(ahead)


def after(value, *others):
    return lax.optimization_barrier((value, others))[0]


VMEM = pl.BlockSpec(memory_space=pltpu.VMEM)
SMEM = pl.BlockSpec(memory_space=pltpu.SMEM)
HBM = pl.BlockSpec(memory_space=pltpu.HBM)


def loop(count, step):
    def run(i, carry):
        step(i)
        return carry

    lax.fori_loop(jnp.int32(0), jnp.int32(count), run, jnp.int32(0))


def add_kernel(a, b, out):
    out[...] = (a[...].astype(F32) + b[...].astype(F32)).astype(BF)


def add(a, b):
    return pl.pallas_call(
        add_kernel,
        in_specs=[VMEM] * 2,
        out_specs=VMEM,
        out_shape=jax.ShapeDtypeStruct(a.shape, BF),
        compiler_params=pltpu.CompilerParams(vmem_limit_bytes=2 << 20),
        cost_estimate=pl.CostEstimate(flops=1 << 20, bytes_accessed=1 << 20, transcendentals=0),
        name="add",
    )(a, b)


def stack_kernel(first, *refs):
    for k in range(4):
        refs[4][lax.rem(first[0] + k, 4)] = refs[k][...]


def stack(first, pieces):
    return pl.pallas_call(
        stack_kernel,
        in_specs=[SMEM] + [VMEM] * 4,
        out_specs=VMEM,
        out_shape=jax.ShapeDtypeStruct((4, 128, 512), BF),
        compiler_params=pltpu.CompilerParams(vmem_limit_bytes=2 << 20),
        cost_estimate=pl.CostEstimate(flops=1 << 20, bytes_accessed=1 << 20, transcendentals=0),
        name="stack",
    )(first, *pieces)


def sum_kernel(*refs):
    for j in range(4):
        total = refs[0][j].astype(F32)
        for k in range(1, 4):
            total += refs[k][j].astype(F32)
        refs[4 + j][...] = total.astype(BF)


def sum_four(blocks):
    return pl.pallas_call(
        sum_kernel,
        in_specs=[VMEM] * 4,
        out_specs=[VMEM] * 4,
        out_shape=[jax.ShapeDtypeStruct((128, 512), BF)] * 4,
        compiler_params=pltpu.CompilerParams(vmem_limit_bytes=4 << 20),
        cost_estimate=pl.CostEstimate(flops=1 << 20, bytes_accessed=1 << 20, transcendentals=0),
        name="sum_four",
    )(*blocks)


def place_of(ids, steps):
    return lax.rem(ids[3] + jnp.where(ids[2] == 0, steps, NZ - steps), NZ)


def load_weight(ids, core, blocks, w, sems, act):
    @pl.when(core == 0)
    def _():
        for i, block in enumerate(blocks):
            act(pltpu.make_async_copy(block, w.at[lax.rem(ids[0] + i, 4), :, 0], sems.at[i]))

    @pl.when(core == 1)
    def _():
        for i, block in enumerate(blocks):
            act(pltpu.make_async_copy(block, w.at[:, lax.rem(ids[1] + i, 4), 1], sems.at[i]))


def weight_rows(ids, k, w):
    zb = place_of(ids, k)
    return w.at[zb // 2, pl.ds(lax.rem(zb, 2) * 2, 2)]


def start(copy):
    copy.start()


def wait(copy):
    copy.wait()


def start(copy):
    copy.start()


def wait(copy):
    copy.wait()


def split_piece(ids, k, piece, mine_ref, cross_ref):
    for core, out in ((ids[2], mine_ref), (1 - ids[2], cross_ref)):
        for xp in range(2):
            lanes = pl.ds(pl.multiple_of(xp * 256 + core * 128, 128), 128)
            out[k, :, xp * 128 : xp * 128 + 128] = piece[:, lanes]


FIRST, NEXT = (0, 1, 7, 2, 6), (3, 5, 4)


def split_kernel(ids, *refs):
    pieces, (mine_ref, cross_ref) = refs[0:5], refs[5:]
    for n, k in enumerate(FIRST):
        split_piece(ids, k, pieces[n], mine_ref, cross_ref)


def split_tokens(ids, pieces):
    return pl.pallas_call(
        split_kernel,
        in_specs=[SMEM] + [VMEM] * 5,
        out_specs=[VMEM] * 2,
        out_shape=[jax.ShapeDtypeStruct((n, 256, 256), BF) for n in (NZ, NZ + 2)],
        compiler_params=pltpu.CompilerParams(vmem_limit_bytes=4 << 20),
        cost_estimate=pl.CostEstimate(flops=1 << 20, bytes_accessed=4 << 20, transcendentals=0),
        name="split_tokens",
    )(ids, *pieces)


def core_term(ids, core, columns, w):
    total = None
    for k in range(NZ):
        rows = weight_rows(ids, k, w)[:, core].reshape(256, 512)
        term = jnp.dot(columns[k], rows, preferred_element_type=F32)
        total = term if total is None else total + term
    return total


def own_kernel(ids, *refs):
    pieces, own, (_, _, acc, w, mine_ref, cross_ref, sems) = refs[0:3], refs[3:7], refs[7:]
    load_weight(ids, ids[2], own, w, sems, start)
    for piece, k in zip(pieces, NEXT):
        split_piece(ids, k, piece, mine_ref, cross_ref)
    load_weight(ids, ids[2], own, w, sems, wait)
    acc[...] = core_term(ids, ids[2], mine_ref, w)


def project_own(ids, pieces, own, mine, cross):
    return pl.pallas_call(
        own_kernel,
        in_specs=[SMEM] + [VMEM] * 3 + [HBM] * 4 + [VMEM] * 2,
        out_specs=[VMEM] * 4,
        out_shape=[
            jax.ShapeDtypeStruct((256, 512), F32),
            jax.ShapeDtypeStruct((4, 4, 2, 128, 512), BF),
            jax.ShapeDtypeStruct(mine.shape, BF),
            jax.ShapeDtypeStruct(cross.shape, BF),
        ],
        input_output_aliases={8: 2, 9: 3},
        scratch_shapes=[pltpu.SemaphoreType.DMA((4,))],
        compiler_params=pltpu.CompilerParams(vmem_limit_bytes=6 << 20),
        cost_estimate=pl.CostEstimate(flops=1 << 32, bytes_accessed=4 << 20, transcendentals=0),
        name="project_own",
    )(ids, *pieces, *own, mine, cross)


def other_kernel(ids, *refs):
    other, (cross, acc, _, dg_ref, p_ref, chip_ref, next_ref, w, sems) = refs[0:4], refs[4:]
    load_weight(ids, 1 - ids[2], other, w, sems, start)
    load_weight(ids, 1 - ids[2], other, w, sems, wait)
    p = (acc[...] + core_term(ids, 1 - ids[2], cross, w)).astype(BF)
    p_ref[...] = p
    tail = p[128:256]
    top = p[0:128].astype(F32)
    head = (dg_ref[0:128].astype(F32) * (top * jax.nn.sigmoid(top))).astype(BF)

    @pl.when(ids[2] == 0)
    def _():
        chip_ref[...], next_ref[...] = tail, head

    @pl.when(ids[2] == 1)
    def _():
        chip_ref[...], next_ref[...] = head, tail


def project_other(ids, other, cross, acc, w, d_gated):
    half = jax.ShapeDtypeStruct((128, 512), BF)
    return pl.pallas_call(
        other_kernel,
        in_specs=[SMEM] + [HBM] * 4 + [VMEM] * 4,
        out_specs=[VMEM] * 4,
        out_shape=[jax.ShapeDtypeStruct((256, 512), BF), half, half, jax.ShapeDtypeStruct(w.shape, BF)],
        input_output_aliases={7: 3},
        scratch_shapes=[pltpu.SemaphoreType.DMA((4,))],
        compiler_params=pltpu.CompilerParams(vmem_limit_bytes=6 << 20),
        cost_estimate=pl.CostEstimate(flops=1 << 30, bytes_accessed=4 << 20, transcendentals=0),
        name="project_other",
    )(ids, *other, cross, acc, w, d_gated)


def mix(ext, live_ref, taps_ref, even, odd, acc, reverse):
    acc[...] = jnp.zeros_like(acc)
    rows = ext.shape[0]
    zero, one = jnp.zeros((), BF), jnp.ones((), BF)

    def shift(b):
        r = ext[...]
        even[...] = r.astype(BF)
        odd[...] = jnp.concatenate([r[8:], r[:8]] if reverse else [r[-8:], r[:-8]], 0).astype(BF)
        ext[...] = pltpu.roll(r, rows - 1 if reverse else 1, 0)
        for u in range(8):
            at = slice(TILE * u, TILE * u + TILE)
            live = live_ref[at] - b.astype(F32).astype(BF)
            sums = []
            for k in range(16):
                v = u + k // 2 if reverse else u + 8 - k // 2
                source = (odd if k % 2 else even)[TILE * v : TILE * v + TILE]
                m = jnp.minimum(jnp.maximum(live - jnp.array(8 * k - 1, BF), zero), one)
                term = source * taps_ref[b, k] * jnp.concatenate([m] * 4, 1)
                level = k
                while level % 2:
                    term = sums.pop() + term
                    level //= 2
                sums.append(term)
            acc[at] += sums[0].astype(F32)

    loop(8, shift)


def gates(p, up, out):
    sigma = jax.nn.sigmoid(p)
    gate = p * sigma
    return (out * gate).astype(BF), up * out * (sigma * (1.0 + p * (1.0 - sigma))), up * gate


LOW, HIGH = slice(0, 128), slice(128, 256)


def inside_kernel(
    p_ref, dg_ref, taps_ref, back_ref, ahead_ref, gated_ref, dgate_ref, part_ref, dconv_ref, ext, even, odd, acc
):
    ext[...] = p_ref[...].astype(F32)
    mix(ext, back_ref.at[HIGH], taps_ref, even, odd, acc, False)
    p, up = p_ref[HIGH].astype(F32), dg_ref[HIGH].astype(F32)
    gated_ref[...], dgate_ref[...], ext[HIGH] = gates(p, up, acc[...])
    p, up = p_ref[LOW].astype(F32), dg_ref[LOW].astype(F32)
    ext[LOW] = up * (p * jax.nn.sigmoid(p))
    dconv_ref[...] = ext[HIGH]
    mix(ext, ahead_ref.at[LOW], taps_ref, even, odd, part_ref, True)


def edges_kernel(
    p_ref, dg_ref, taps_ref, back_ref, ahead_ref, chip_ref, next_ref, gated_hi, dgate_ref, part_ref, dconv_ref,
    ids, w_ref, _, gated_ref, dproj_ref, far_ref, w, cross_ref, ext, even, odd, acc, sem,
):
    load = pltpu.make_async_copy(w_ref, w, sem)
    load.start()
    p, up = p_ref[LOW].astype(F32), dg_ref[LOW].astype(F32)
    from_chip, from_next = chip_ref[...].astype(F32), next_ref[...].astype(F32)
    ext[LOW] = jnp.where(ids[2] == 0, from_next, from_chip)
    ext[HIGH] = p
    mix(ext, back_ref.at[LOW], taps_ref, even, odd, acc, False)
    gated_ref[LOW], d_gate, _ = gates(p, up, acc[...])
    gated_ref[HIGH] = gated_hi[...]
    dproj_ref[LOW] = (part_ref[...] + d_gate).astype(BF)
    ext[LOW] = dconv_ref[...]
    from_chip, from_next = chip_ref[...].astype(F32), next_ref[...].astype(F32)
    ext[HIGH] = jnp.where(ids[2] == 0, from_chip, from_next)
    mix(ext, ahead_ref.at[HIGH], taps_ref, even, odd, acc, True)
    dproj_ref[HIGH] = (acc[...] + dgate_ref[...]).astype(BF)
    cross_ref[NZ] = dproj_ref[:, 0:256]
    cross_ref[NZ + 1] = dproj_ref[:, 256:512]
    load.wait()
    far_ref[...] = back_term(dproj_ref[...], weight_rows(ids, 4, w)[...].reshape(512, 512))


def back_term(d, block):
    return lax.dot_general(d, block, (((1,), (1,)), ((), ())), preferred_element_type=F32).astype(BF)


def mix_call(kernel, name, shapes, *operands, specs=None, scratch=(), aliases={}):
    return pl.pallas_call(
        kernel,
        in_specs=specs or [VMEM] * len(operands),
        out_specs=[VMEM] * len(shapes),
        out_shape=[jax.ShapeDtypeStruct(shape, kind) for shape, kind in shapes],
        scratch_shapes=[
            pltpu.VMEM((256, 512), F32),
            pltpu.VMEM((256, 512), BF),
            pltpu.VMEM((256, 512), BF),
            pltpu.VMEM((128, 512), F32),
            *scratch,
        ],
        input_output_aliases=aliases,
        compiler_params=pltpu.CompilerParams(vmem_limit_bytes=8 << 20),
        cost_estimate=pl.CostEstimate(flops=1 << 32, bytes_accessed=4 << 20, transcendentals=0),
        name=name,
    )(*operands)


def conv(ids, p, for_chip, for_next, d_gated, taps, back, ahead, w, cross):
    half, whole = (128, 512), (256, 512)
    halos = to_other_core(for_chip), to_next_chip(for_next)
    inside = mix_call(
        inside_kernel, "inside", [(half, BF), (half, F32), (half, F32), (half, F32)], p, d_gated, taps, back, ahead
    )
    return mix_call(
        edges_kernel, "edges", [(whole, BF), (whole, BF), (whole, BF), (w.shape, BF), (cross.shape, BF)],
        p, d_gated, taps, back, ahead, *halos, *inside, ids, w, cross,
        specs=[VMEM] * 11 + [SMEM, HBM, VMEM], scratch=[pltpu.SemaphoreType.DMA], aliases={13: 4},
    )


def near_kernel(order, ids, d_ref, w, *outs):
    d = d_ref[...]
    for steps, out in zip(order, outs):
        out[...] = back_term(d, weight_rows(ids, steps, w)[...].reshape(512, 512))


def near_terms(ids, d_proj, weight, order, flops):
    return pl.pallas_call(
        functools.partial(near_kernel, order),
        in_specs=[SMEM, VMEM, VMEM],
        out_specs=[VMEM] * len(order),
        out_shape=[jax.ShapeDtypeStruct((256, 512), BF)] * len(order),
        compiler_params=pltpu.CompilerParams(vmem_limit_bytes=4 << 20),
        cost_estimate=pl.CostEstimate(flops=flops, bytes_accessed=len(order) << 20, transcendentals=0),
        name="near_terms",
    )(ids, d_proj, weight)


def add_three_kernel(a, b, c, out):
    out[...] = (a[...].astype(F32) + b[...].astype(F32) + c[...].astype(F32)).astype(BF)


def add_three(a, b, c):
    return pl.pallas_call(
        add_three_kernel,
        in_specs=[VMEM] * 3,
        out_specs=VMEM,
        out_shape=jax.ShapeDtypeStruct(a.shape, BF),
        compiler_params=pltpu.CompilerParams(vmem_limit_bytes=2 << 20),
        cost_estimate=pl.CostEstimate(flops=1 << 34, bytes_accessed=1 << 20, transcendentals=0),
        name="add_three",
    )(a, b, c)


def grad_kernel(ids, mine, theirs, d_mine, *refs):
    outs, out, d_theirs = refs[:4], refs[4], refs[5]
    d_theirs[:, 0:256] = theirs[NZ]
    d_theirs[:, 256:512] = theirs[NZ + 1]
    me = ids[2]
    dims = (((0,), (0,)), ((), ()))
    for k in range(NZ):
        zb = place_of(ids, k)
        total = lax.dot_general(mine[k], d_mine[...], dims, preferred_element_type=F32)
        total += lax.dot_general(theirs[(NZ - k) % NZ], d_theirs[...], dims, preferred_element_type=F32)
        total = total.astype(BF)
        for xp in range(2):
            dy = lax.rem(zb // 2 + 4 - ids[0], 4)
            dx = lax.rem(lax.rem(zb, 2) * 2 + xp + 4 - ids[1], 4)
            out[jnp.where(me == 0, dy, dx), jnp.where(me == 0, dx, dy)] = total[xp * 128 : xp * 128 + 128]
    for k in range(4):
        outs[k][...] = out[k]


def weight_terms(ids, mine, theirs, d_mine):
    return pl.pallas_call(
        grad_kernel,
        in_specs=[SMEM] + [VMEM] * 3,
        out_specs=[VMEM] * 4,
        out_shape=[jax.ShapeDtypeStruct((4, 128, 512), BF)] * 4,
        scratch_shapes=[pltpu.VMEM((4, 4, 128, 512), BF), pltpu.VMEM((256, 512), BF)],
        compiler_params=pltpu.CompilerParams(vmem_limit_bytes=6 << 20),
        cost_estimate=pl.CostEstimate(flops=2 * 512 * 2048 * 512, bytes_accessed=5 << 20, transcendentals=0),
        name="weight_terms",
    )(ids, mine, theirs, d_mine)


def sum_up(ids, d_proj, far, weight, mine, cross):
    p = around_z(far, 1)
    theirs = to_other_core(cross)
    p3, q3 = near_terms(ids, d_proj, weight, (3, 5), 1 << 28)
    q = around_z(q3, -1)
    g = weight_terms(ids, mine, after(theirs, q3), d_proj)
    p2, q2, p1, q1, own = near_terms(ids, after(d_proj, g[0]), weight, (2, 6, 1, 7, 0), 1 << 33)
    p = around_z(add(after(p3, own), p), 1)
    s = [g[0]] + [wide(g[k], k) for k in (1, 2, 3)]
    q = around_z(add(q2, q), -1)
    p = around_z(add(p2, p), 1)
    q_last = add(q1, q)
    q = around_z(q_last, -1)
    p_last = add(p1, p)
    p = around_z(p_last, 1)
    n = sum_four([after(s[0], p_last, q_last)] + s[1:])
    n = [n[0]] + [narrow(n[k], k) for k in (1, 2, 3)]
    d_tokens = add_three(own, p, q)
    return d_tokens, sum(v.astype(F32) for v in after(n, d_tokens))


def body(tokens, contig_lengths, w_in, conv_filter, d_gated):
    rows = tokens.shape[0]
    seq_total = rows * NY * NX * NC
    row, z = lax.axis_index("row"), lax.axis_index("col")
    core, chip = row % NC, row // NC
    y, x = chip // NX, chip % NX
    ids = jnp.stack([y, x, core, z]).astype(jnp.int32)

    w = [narrow(w_in, 4 - k) for k in (1, 2, 3)]
    p1, q1 = around_z(tokens, 1), around_z(tokens, -1)
    first = jnp.where(core == 0, x, y).astype(jnp.int32).reshape(1)
    row_block = stack(first, [w_in] + w)
    own = [row_block] + [wide(row_block, 4 - k) for k in (1, 2, 3)]
    p2, q2 = around_z(after(p1, row_block), 1), around_z(after(q1, row_block), -1)
    conv_filter, contig_lengths = after((conv_filter, contig_lengths), q1)
    back, ahead = live_taps(contig_lengths, row * rows, rows)
    taps = conv_filter.astype(BF).reshape(16, 8, 1, 512).transpose(1, 0, 2, 3)
    taps = jnp.broadcast_to(taps, (8, 16, TILE, 512))
    p3, q3 = around_z(p2, 1), around_z(q2, -1)
    mine, cross = split_tokens(ids, [tokens, q1, p1, q2, p2])
    p4 = around_z(after(p3, own), 1)
    other = [to_other_core(block) for block in after(own, back, ahead, taps, mine)]
    acc, weight, mine, cross = project_own(ids, [q3, p3, p4], own, mine, cross)
    projected, for_chip, for_next, weight = project_other(ids, other, cross, acc, weight, d_gated)
    gated, d_proj, far, weight, cross = conv(
        ids, projected, for_chip, for_next, d_gated, taps, back, ahead, weight, cross
    )
    d_tokens, grad = sum_up(ids, d_proj, far, weight, mine, cross)
    return gated, d_tokens, grad * (1.0 / math.sqrt(seq_total))


def solution(mesh):
    placed = (P("row", "col"), P(), P("row", "col"), P(None, "col"), P("row", "col"))
    return jax.shard_map(
        body,
        mesh=mesh,
        in_specs=placed,
        out_specs=(P("row", "col"), P("row", "col"), P("row", "col")),
        check_vma=False,
    )
```
